512 devices in a mesh: depth: 32 (over x_lo, y, core), height: 16 (over x_hi, z).
Axes of the slice: x: 4 (x_hi: 2, x_lo: 2; x = x_hi * 2 + x_lo), y: 8, z: 8, core: 2. Of those that a mesh axis runs over, the one named last changes fastest.
Arguments:
- volume: bfloat16 [4, 128, 128, 512], P(None, 'depth', 'height'), may hold values from -6 to 6
- first_kernel: bfloat16 [3, 3, 3, 4, 32], replicated, may hold values from -1.25 to 1.25
- second_kernel: bfloat16 [3, 3, 3, 32, 64], replicated, may hold values from -0.4375 to 0.4375
- third_kernel: bfloat16 [3, 3, 3, 64, 128], replicated, may hold values from -0.3125 to 0.3125
Outputs:
- features: bfloat16 [128, 32, 32, 128], P(None, 'depth', 'height')
The draws below stay inside these ranges and needn't reach their ends.
All inputs are finite; a program needn't handle non-finite values.
Results may differ from the reference program's by a relative error of at most 0.013.
Values may be sent and summed in bfloat16 or wider, within the bound.
A program may use at most 64 MiB of HBM per device.

```python
import jax
import jax.numpy as jnp
from jax import lax

C0 = 4
C1 = 32
C2 = 64
C3 = 128
W = 512
DEPTH = 128
HEIGHT = 128
SLICE = 4


def levels(stream_key, dims, cuts, low, high):
    factor_of, own = 1.0, jax.random.fold_in(stream_key, 6)
    for dim, shards_of in cuts:
        heights = jnp.exp(jax.random.uniform(jax.random.fold_in(own, dim), (shards_of,), jnp.float32, low / len(cuts), high / len(cuts)))
        factor_of = factor_of * jnp.repeat(heights, dims[dim] // shards_of).reshape([-1 if axis == dim else 1 for axis in range(len(dims))])
    return factor_of


def bell_draw(own_key, dims, spread, limit, shards=(), kind=jnp.bfloat16):
    array = spread * jax.random.normal(own_key, dims, jnp.float32)
    if shards:
        array = array * levels(own_key, dims, shards, -0.22, 0.18)
    return jnp.clip(array, -limit, limit).astype(kind)


def setup_inputs(seed: int = 0) -> dict:
    arg_keys = jax.random.split(jax.random.key(seed), 5)
    return {
        "volume": bell_draw(arg_keys[0], (C0, DEPTH, HEIGHT, W), 1.0, 6.0, ((1, 32), (2, 16))),
        "first_kernel": bell_draw(arg_keys[1], (3, 3, 3, C0, C1), (27 * C0 // 4) ** -0.5, 1.25),
        "second_kernel": bell_draw(arg_keys[2], (3, 3, 3, C1, C2), (27 * C1 // 4) ** -0.5, 0.4375),
        "third_kernel": bell_draw(arg_keys[3], (3, 3, 3, C2, C3), (27 * C2 // 4) ** -0.5, 0.3125),
    }


slope = 0.3


def leaky_relu(values):
    return jnp.where(values > 0, values, slope * values)


def pool_pairs(values):
    channels, deep_size, tall_size, wide_size = values.shape
    blocks = values.reshape(channels, deep_size // 2, 2, tall_size // 2, 2, wide_size // 2, 2)
    return jnp.max(blocks, axis=(2, 4, 6))


def convolve(field, kernel, depth_pad):
    result = lax.conv_general_dilated(field[None], kernel, (1, 1, 1), ((depth_pad, depth_pad), (1, 1), (1, 1)), dimension_numbers=("NCDHW", "DHWIO", "NCDHW"), precision=lax.Precision.HIGHEST)
    return result[0]


def conv_layer(field, kernel):
    deep_size = field.shape[1]
    padded = jnp.pad(field, ((0, 0), (1, 1), (0, 0), (0, 0)))
    weights = kernel.astype(jnp.float32)

    def one_block(index):
        offset = (index * 2).astype(jnp.int32)
        piece = lax.dynamic_slice_in_dim(padded, offset, 4, 1).astype(jnp.float32)
        return pool_pairs(leaky_relu(convolve(piece, weights, 0))).astype(jnp.bfloat16)

    blocks = lax.map(one_block, jnp.arange(deep_size // 2, dtype=jnp.int32))
    return jnp.moveaxis(blocks[:, :, 0], 0, 1)


def reference(volume, first_kernel, second_kernel, third_kernel):
    pooled_one = conv_layer(volume, first_kernel)
    pooled_two = conv_layer(pooled_one, second_kernel)
    field = pooled_two.astype(jnp.float32)
    weights = third_kernel.astype(jnp.float32)

    def add_slice(index, total):
        offset = (index * SLICE).astype(jnp.int32)
        part_field = lax.dynamic_slice_in_dim(field, offset, SLICE, 0)
        part_kernel = lax.dynamic_slice_in_dim(weights, offset, SLICE, 3)
        partial_sum = convolve(part_field, part_kernel, 1).astype(jnp.bfloat16)
        return total + partial_sum.astype(jnp.float32)

    initial = jnp.zeros((C3, field.shape[1], field.shape[2], field.shape[3]), jnp.float32)
    total = lax.fori_loop(0, C2 // SLICE, add_slice, initial)
    return leaky_relu(total).astype(jnp.bfloat16)
```

```python
import functools

import jax
import jax.numpy as jnp
import numpy as np
from jax import lax
from jax.experimental import pallas as pl
from jax.experimental.pallas import tpu as pltpu
from jax.sharding import PartitionSpec as P

MESH = pl.DeviceIdType.MESH
BF16 = jnp.bfloat16
F32 = jnp.float32
SLOPE = 0.3
SIDES = [(a, b) for a in (-1, 0, 1) for b in (-1, 0, 1) if (a, b) != (0, 0)]


def phase_matrix():
    matrix = np.zeros((512, 4, 128), np.float32)
    for t in range(4):
        for l in range(128):
            matrix[4 * l + t, t, l] = 1
    return matrix.reshape(512, 512)


def first_placement():
    place = np.zeros((3, 3, 3, 4, 2, 2, 2, 2, 4, 4, 4, 4), np.float32)
    order = ((1, 2, 3, 0), (3, 0, 1, 2))
    for a, b, e, c, s, pd, ph, pw in np.ndindex(3, 3, 3, 4, 2, 2, 2, 2):
        place[a, b, e, c, s, pd, ph, pw, pd + a, ph + b, order[s].index(pw + e), c] = 1
    return np.pad(place.reshape(108, 4096), ((0, 20), (0, 0)))


def nt_dot(left, right):
    return lax.dot_general(left, right, (((1,), (1,)), ((), ())), preferred_element_type=F32)


def dot(left, right):
    return jnp.dot(left, right, preferred_element_type=F32)


def eye(size):
    rows = lax.broadcasted_iota(jnp.int32, (size, size), 0)
    columns = lax.broadcasted_iota(jnp.int32, (size, size), 1)
    return jnp.where(rows == columns, 1.0, 0.0).astype(BF16)


def before(value):
    lane = lax.broadcasted_iota(jnp.int32, value.shape, 1)
    return jnp.where(lane == 0, 0.0, pltpu.roll(value, 1, 1))


def after(value):
    lane = lax.broadcasted_iota(jnp.int32, value.shape, 1)
    return jnp.where(lane == 127, 0.0, pltpu.roll(value, 127, 1))


def leaky(value):
    return jnp.where(value > 0, value, SLOPE * value)


def span(shift, size, halo, received):
    if shift == 0:
        return pl.ds(halo, size)
    if received:
        return pl.ds(0, halo) if shift == 1 else pl.ds(halo + size, halo)
    return pl.ds(size, halo) if shift == 1 else pl.ds(halo, halo)


def body(
    depths, heights,
    volume, first, second, third, phases, placement, out,
    x, k1, k2, k3, phase, place, y, g, e0, e1, k1f, w1, f, w2, t, u, w3, of, ob,
    load_sem, send_sem, recv_sem,
):
    di, hi = lax.axis_index("depth"), lax.axis_index("height")

    def within(a, b):
        return (di + a >= 0) & (di + a < depths) & (hi + b >= 0) & (hi + b < heights)

    loads = [
        pltpu.make_async_copy(source, target, load_sem.at[i])
        for i, (source, target) in enumerate(
            ((volume, x), (phases, phase), (first, k1), (placement, place), (second, k2), (third, k3))
        )
    ]
    for load in loads:
        load.start()

    barrier = pltpu.get_barrier_semaphore()
    for a, b in SIDES:
        @pl.when(within(a, b))
        def _():
            pl.semaphore_signal(barrier, inc=1, device_id=(di + a, hi + b), device_id_type=MESH)

    for a, b in SIDES:
        @pl.when(jnp.logical_not(within(-a, -b)))
        def _():
            d1, h1 = span(a, 4, 3, True), span(b, 8, 3, True)
            g[d1, h1] = jnp.zeros((d1.size, h1.size, 16, 128), BF16)
            d2, h2 = span(a, 1, 1, True), span(b, 2, 1, True)
            t[d2, h2] = jnp.zeros((d2.size, h2.size, 64, 128), BF16)

    loads[0].wait()
    loads[1].wait()
    spread = dot(x[...].reshape(128, 512), phase[...])
    for i in range(4):
        y[pl.ds(i * 128, 128), :] = spread[:, i * 128 : (i + 1) * 128]
    for d in range(4):
        for h in range(8):
            g[3 + d, 3 + h] = y[pl.ds(d * 8 + h, 16, stride=32), :].astype(BF16)

    count_d = 1 + (di > 0).astype(jnp.int32) + (di < depths - 1).astype(jnp.int32)
    count_h = 1 + (hi > 0).astype(jnp.int32) + (hi < heights - 1).astype(jnp.int32)
    pl.semaphore_wait(barrier, count_d * count_h - 1)

    def exchange(buffer, depth_size, height_size, halo, base):
        for i, (a, b) in enumerate(SIDES):
            copy = pltpu.make_async_remote_copy(
                src_ref=buffer.at[span(a, depth_size, halo, False), span(b, height_size, halo, False)],
                dst_ref=buffer.at[span(a, depth_size, halo, True), span(b, height_size, halo, True)],
                send_sem=send_sem.at[base + i],
                recv_sem=recv_sem.at[base + i],
                device_id=(di + a, hi + b),
                device_id_type=MESH,
            )
            yield (a, b), copy

    def start(buffer, depth_size, height_size, halo, base):
        for (a, b), copy in exchange(buffer, depth_size, height_size, halo, base):
            pl.when(within(a, b))(copy.start)

    def arrive(buffer, depth_size, height_size, halo, base):
        for (a, b), copy in exchange(buffer, depth_size, height_size, halo, base):
            pl.when(within(-a, -b))(copy.wait_recv)

    def sent(buffer, depth_size, height_size, halo, base):
        for (a, b), copy in exchange(buffer, depth_size, height_size, halo, base):
            pl.when(within(a, b))(copy.wait_send)

    start(g, 4, 8, 3, 0)

    for load in loads[2:]:
        load.wait()
    k1f[...] = jnp.zeros_like(k1f)
    for i, (a, b, e) in enumerate(np.ndindex(3, 3, 3)):
        k1f[pl.ds(4 * i, 4), :] = k1[a, b, e].astype(F32)
    flat = nt_dot(eye(32), k1f[...].astype(BF16)).astype(BF16)
    for s in range(2):
        for p in range(0, 8, 4):
            wide = dot(flat, place[:, pl.ds((s * 8 + p) * 256, 1024)]).astype(BF16)
            for q in range(4):
                w1[s, pl.ds((p + q) * 32, 32), :] = wide[:, q * 256 : (q + 1) * 256]

    unit = eye(64)
    blank = jnp.zeros((32, 64), BF16)
    for a in range(3):
        for b in range(3):
            taps = k2[a, b].reshape(96, 64)
            turned = nt_dot(unit, jnp.concatenate([taps, blank, blank, taps], 0)).astype(BF16)
            for ph in range(2):
                for pw in range(2):
                    w2[pl.ds(ph * 128 + pw * 64, 64), pl.ds((a * 4 + b + ph) * 128, 128)] = turned[
                        :, pw * 128 : (pw + 1) * 128
                    ]
        for ph, h in ((0, 3), (1, 0)):
            w2[pl.ds(ph * 128, 128), pl.ds((a * 4 + h) * 128, 128)] = jnp.zeros((128, 128), BF16)

    unit = eye(128)
    for i in range(9):
        rows = k3[i // 3, i % 3].reshape(192, 128)
        w3[i] = nt_dot(unit, rows).astype(BF16)

    arrive(g, 4, 8, 3, 0)

    @pl.loop(0, 10)
    def _(d):
        value = g[d].astype(F32)
        low, high = value[:, 0:8].reshape(112, 128), value[:, 8:16].reshape(112, 128)
        row = lax.broadcasted_iota(jnp.int32, (112, 128), 0) & 7
        turned = jnp.where(row >= 4, before(high), high)
        e0[d] = jnp.concatenate([value[:, 0:8], turned.reshape(14, 8, 128)], 1).astype(BF16)
        turned = jnp.where(row < 4, after(low), low)
        e1[d] = jnp.concatenate([turned.reshape(14, 8, 128), value[:, 8:16]], 1).astype(BF16)

    @pl.loop(0, 4)
    def _(dp):
        deep = 2 * di + dp - 1
        deep_in = (deep >= 0) & (deep < 2 * depths)
        for hp in range(0, 6, 2):
            halves = []
            for s, e in enumerate((e0, e1)):
                parts = [
                    e[pl.ds(2 * dp, 4), pl.ds(2 * (hp + j), 4)].reshape(256, 128) for j in range(2)
                ]
                sums = dot(w1[s], jnp.concatenate(parts, 1))
                halves.append(leaky(jnp.max(sums.reshape(8, 32, 256), axis=0)))
            for j in range(2):
                tall = 4 * hi + hp + j - 1
                keep = jnp.where(deep_in & (tall >= 0) & (tall < 4 * heights), 1.0, 0.0)
                p0, p1 = (half[:, j * 128 : (j + 1) * 128] * keep for half in halves)
                for i, part in enumerate((before(p1), p0, p1, after(p0))):
                    f[dp, hp + j, pl.ds(32 * i, 32), :] = part.astype(BF16)

    best = None
    for pd in range(2):
        parts = [f[pl.ds(pd, 3), pl.ds(2 * j, 4)].reshape(1536, 128) for j in range(2)]
        sums = dot(w2[...], jnp.concatenate(parts, 1))
        sums = jnp.max(sums.reshape(4, 64, 256), axis=0)
        best = sums if best is None else jnp.maximum(best, sums)
    best = leaky(best).astype(BF16)
    t[1, 1] = best[:, 0:128]
    t[1, 2] = best[:, 128:256]
    start(t, 1, 2, 1, 8)
    arrive(t, 1, 2, 1, 8)

    for d in range(3):
        for h in range(4):
            value = t[d, h].astype(F32)
            u[d, h, pl.ds(0, 64), :] = before(value).astype(BF16)
            u[d, h, pl.ds(64, 64), :] = t[d, h]
            u[d, h, pl.ds(128, 64), :] = after(value).astype(BF16)
    total = None
    for i in range(9):
        parts = [u[i // 3, i % 3 + j] for j in range(2)]
        term = dot(w3[i], jnp.concatenate(parts, 1))
        total = term if total is None else total + term
    total = leaky(total)
    of[pl.ds(0, 128, stride=2), :] = total[:, 0:128]
    of[pl.ds(1, 128, stride=2), :] = total[:, 128:256]
    ob[...] = of[...].astype(BF16)
    store = pltpu.make_async_copy(ob, out, load_sem.at[0])
    store.start()
    sent(g, 4, 8, 3, 0)
    sent(t, 1, 2, 1, 8)
    store.wait()


def shards(depths, heights, volume, first, second, third):
    phases = jnp.asarray(phase_matrix(), BF16)
    placement = jnp.asarray(first_placement(), BF16)
    result = pl.pallas_call(
        functools.partial(body, depths, heights),
        out_shape=jax.ShapeDtypeStruct((256, 128), BF16),
        in_specs=[pl.BlockSpec(memory_space=pl.ANY)] * 6,
        out_specs=pl.BlockSpec(memory_space=pl.ANY),
        scratch_shapes=[
            pltpu.VMEM((4, 4, 8, 512), BF16),
            pltpu.VMEM((3, 3, 3, 4, 32), BF16),
            pltpu.VMEM((3, 3, 96, 64), BF16),
            pltpu.VMEM((3, 3, 192, 128), BF16),
            pltpu.VMEM((512, 512), BF16),
            pltpu.VMEM((128, 4096), BF16),
            pltpu.VMEM((512, 128), F32),
            pltpu.VMEM((10, 14, 16, 128), BF16),
            pltpu.VMEM((10, 14, 16, 128), BF16),
            pltpu.VMEM((10, 14, 16, 128), BF16),
            pltpu.VMEM((128, 32), F32),
            pltpu.VMEM((2, 256, 256), BF16),
            pltpu.VMEM((4, 6, 128, 128), BF16),
            pltpu.VMEM((256, 1536), BF16),
            pltpu.VMEM((3, 4, 64, 128), BF16),
            pltpu.VMEM((3, 4, 192, 128), BF16),
            pltpu.VMEM((9, 128, 192), BF16),
            pltpu.VMEM((256, 128), F32),
            pltpu.VMEM((256, 128), BF16),
            pltpu.SemaphoreType.DMA((6,)),
            pltpu.SemaphoreType.DMA((16,)),
            pltpu.SemaphoreType.DMA((16,)),
        ],
        compiler_params=pltpu.CompilerParams(
            collective_id=0, has_side_effects=True, vmem_limit_bytes=48 * 2**20
        ),
        cost_estimate=pl.CostEstimate(flops=2 * 10**9, bytes_accessed=3 * 10**6, transcendentals=0),
        name="layers",
    )(volume, first, second.reshape(3, 3, 96, 64), third.reshape(3, 3, 192, 128), phases, placement)
    return result.reshape(128, 1, 2, 128)


def solution(mesh):
    in_specs = (P(None, "depth", "height", None), P(), P(), P())
    out_specs = P(None, "depth", "height", None)
    local = functools.partial(shards, mesh.shape["depth"], mesh.shape["height"])
    return jax.shard_map(local, mesh=mesh, in_specs=in_specs, out_specs=out_specs, check_vma=False)
```

```python
import functools

import jax
import jax.numpy as jnp
import numpy as np
from jax import lax
from jax.experimental import pallas as pl
from jax.experimental.pallas import tpu as pltpu
from jax.sharding import PartitionSpec as P

MESH = pl.DeviceIdType.MESH
BF16 = jnp.bfloat16
F32 = jnp.float32
SLOPE = 0.3
SIDES = [(a, b) for a in (-1, 0, 1) for b in (-1, 0, 1) if (a, b) != (0, 0)]


def phase_matrix():
    matrix = np.zeros((512, 4, 128), np.float32)
    for t in range(4):
        for l in range(128):
            matrix[4 * l + t, t, l] = 1
    return matrix.reshape(512, 512)


def first_placement():
    place = np.zeros((3, 3, 3, 4, 2, 2, 2, 2, 4, 4, 4, 4), np.float32)
    order = ((1, 2, 3, 0), (3, 0, 1, 2))
    for a, b, e, c, s, pd, ph, pw in np.ndindex(3, 3, 3, 4, 2, 2, 2, 2):
        place[a, b, e, c, s, pd, ph, pw, pd + a, ph + b, order[s].index(pw + e), c] = 1
    return np.pad(place.reshape(108, 4096), ((0, 20), (0, 0)))


def nt_dot(left, right):
    return lax.dot_general(left, right, (((1,), (1,)), ((), ())), preferred_element_type=F32)


def dot(left, right):
    return jnp.dot(left, right, preferred_element_type=F32)


def eye(size):
    rows = lax.broadcasted_iota(jnp.int32, (size, size), 0)
    columns = lax.broadcasted_iota(jnp.int32, (size, size), 1)
    return jnp.where(rows == columns, 1.0, 0.0).astype(BF16)


def before(value):
    lane = lax.broadcasted_iota(jnp.int32, value.shape, 1)
    return jnp.where(lane == 0, 0.0, pltpu.roll(value, 1, 1))


def after(value):
    lane = lax.broadcasted_iota(jnp.int32, value.shape, 1)
    return jnp.where(lane == 127, 0.0, pltpu.roll(value, 127, 1))


def leaky(value):
    return jnp.where(value > 0, value, SLOPE * value)


def span(shift, size, halo, received):
    if shift == 0:
        return pl.ds(halo, size)
    if received:
        return pl.ds(0, halo) if shift == 1 else pl.ds(halo + size, halo)
    return pl.ds(size, halo) if shift == 1 else pl.ds(halo, halo)


def body(
    depths, heights,
    volume, first, second, third, phases, placement, out,
    x, k1, k2, k3, phase, place, y, g, e0, e1, k1f, w1, f, w2, t, u, w3, of, ob,
    load_sem, send_sem, recv_sem,
):
    di, hi = lax.axis_index("depth"), lax.axis_index("height")

    def within(a, b):
        return (di + a >= 0) & (di + a < depths) & (hi + b >= 0) & (hi + b < heights)

    loads = [
        pltpu.make_async_copy(source, target, load_sem.at[i])
        for i, (source, target) in enumerate(
            ((volume, x), (phases, phase), (first, k1), (placement, place), (second, k2), (third, k3))
        )
    ]
    for load in loads:
        load.start()

    barrier = pltpu.get_barrier_semaphore()
    for a, b in SIDES:
        @pl.when(within(a, b))
        def _():
            pl.semaphore_signal(barrier, inc=1, device_id=(di + a, hi + b), device_id_type=MESH)

    for a, b in SIDES:
        @pl.when(jnp.logical_not(within(-a, -b)))
        def _():
            d1, h1 = span(a, 4, 3, True), span(b, 8, 3, True)
            g[d1, h1] = jnp.zeros((d1.size, h1.size, 16, 128), BF16)
            d2, h2 = span(a, 1, 1, True), span(b, 2, 1, True)
            t[d2, h2] = jnp.zeros((d2.size, h2.size, 64, 128), BF16)

    loads[0].wait()
    loads[1].wait()
    spread = dot(x[...].reshape(128, 512), phase[...])
    for i in range(4):
        y[pl.ds(i * 128, 128), :] = spread[:, i * 128 : (i + 1) * 128]
    for d in range(4):
        for h in range(8):
            g[3 + d, 3 + h] = y[pl.ds(d * 8 + h, 16, stride=32), :].astype(BF16)

    count_d = 1 + (di > 0).astype(jnp.int32) + (di < depths - 1).astype(jnp.int32)
    count_h = 1 + (hi > 0).astype(jnp.int32) + (hi < heights - 1).astype(jnp.int32)
    pl.semaphore_wait(barrier, count_d * count_h - 1)

    def exchange(buffer, depth_size, height_size, halo, base):
        for i, (a, b) in enumerate(SIDES):
            copy = pltpu.make_async_remote_copy(
                src_ref=buffer.at[span(a, depth_size, halo, False), span(b, height_size, halo, False)],
                dst_ref=buffer.at[span(a, depth_size, halo, True), span(b, height_size, halo, True)],
                send_sem=send_sem.at[base + i],
                recv_sem=recv_sem.at[base + i],
                device_id=(di + a, hi + b),
                device_id_type=MESH,
            )
            yield (a, b), copy

    def start(buffer, depth_size, height_size, halo, base):
        for (a, b), copy in exchange(buffer, depth_size, height_size, halo, base):
            pl.when(within(a, b))(copy.start)

    def arrive(buffer, depth_size, height_size, halo, base):
        for (a, b), copy in exchange(buffer, depth_size, height_size, halo, base):
            pl.when(within(-a, -b))(copy.wait_recv)

    def sent(buffer, depth_size, height_size, halo, base):
        for (a, b), copy in exchange(buffer, depth_size, height_size, halo, base):
            pl.when(within(a, b))(copy.wait_send)

    start(g, 4, 8, 3, 0)

    for load in loads[2:]:
        load.wait()
    k1f[...] = jnp.zeros_like(k1f)
    for i, (a, b, e) in enumerate(np.ndindex(3, 3, 3)):
        k1f[pl.ds(4 * i, 4), :] = k1[a, b, e].astype(F32)
    flat = nt_dot(eye(32), k1f[...].astype(BF16)).astype(BF16)
    for s in range(2):
        for p in range(0, 8, 4):
            wide = dot(flat, place[:, pl.ds((s * 8 + p) * 256, 1024)]).astype(BF16)
            for q in range(4):
                w1[s, pl.ds((p + q) * 32, 32), :] = wide[:, q * 256 : (q + 1) * 256]

    unit = eye(64)
    blank = jnp.zeros((32, 64), BF16)
    for a in range(3):
        for b in range(3):
            taps = k2[a, b].reshape(96, 64)
            turned = nt_dot(unit, jnp.concatenate([taps, blank, blank, taps], 0)).astype(BF16)
            for ph in range(2):
                for pw in range(2):
                    w2[pl.ds(ph * 128 + pw * 64, 64), pl.ds((a * 4 + b + ph) * 128, 128)] = turned[
                        :, pw * 128 : (pw + 1) * 128
                    ]
        for ph, h in ((0, 3), (1, 0)):
            w2[pl.ds(ph * 128, 128), pl.ds((a * 4 + h) * 128, 128)] = jnp.zeros((128, 128), BF16)

    unit = eye(128)
    for i in range(9):
        rows = k3[i // 3, i % 3].reshape(192, 128)
        w3[i] = nt_dot(unit, rows).astype(BF16)

    arrive(g, 4, 8, 3, 0)

    @pl.loop(0, 10)
    def _(d):
        value = g[d].astype(F32)
        low, high = value[:, 0:8].reshape(112, 128), value[:, 8:16].reshape(112, 128)
        row = lax.broadcasted_iota(jnp.int32, (112, 128), 0) & 7
        turned = jnp.where(row >= 4, before(high), high)
        e0[d] = jnp.concatenate([value[:, 0:8], turned.reshape(14, 8, 128)], 1).astype(BF16)
        turned = jnp.where(row < 4, after(low), low)
        e1[d] = jnp.concatenate([turned.reshape(14, 8, 128), value[:, 8:16]], 1).astype(BF16)

    @pl.loop(0, 4)
    def _(dp):
        deep = 2 * di + dp - 1
        deep_in = (deep >= 0) & (deep < 2 * depths)
        for hp in range(0, 6, 2):
            halves = []
            for s, e in enumerate((e0, e1)):
                parts = [
                    e[pl.ds(2 * dp, 4), pl.ds(2 * (hp + j), 4)].reshape(256, 128) for j in range(2)
                ]
                sums = dot(w1[s], jnp.concatenate(parts, 1))
                halves.append(leaky(jnp.max(sums.reshape(8, 32, 256), axis=0)))
            for j in range(2):
                tall = 4 * hi + hp + j - 1
                keep = jnp.where(deep_in & (tall >= 0) & (tall < 4 * heights), 1.0, 0.0)
                p0, p1 = (half[:, j * 128 : (j + 1) * 128] * keep for half in halves)
                for i, part in enumerate((before(p1), p0, p1, after(p0))):
                    f[dp, hp + j, pl.ds(32 * i, 32), :] = part.astype(BF16)

    best = None
    for pd in range(2):
        parts = [f[pl.ds(pd, 3), pl.ds(2 * j, 4)].reshape(1536, 128) for j in range(2)]
        sums = dot(w2[...], jnp.concatenate(parts, 1))
        sums = jnp.max(sums.reshape(4, 64, 256), axis=0)
        best = sums if best is None else jnp.maximum(best, sums)
    best = leaky(best).astype(BF16)
    t[1, 1] = best[:, 0:128]
    t[1, 2] = best[:, 128:256]
    start(t, 1, 2, 1, 8)
    arrive(t, 1, 2, 1, 8)

    for d in range(3):
        for h in range(4):
            value = t[d, h].astype(F32)
            u[d, h, pl.ds(0, 64), :] = before(value).astype(BF16)
            u[d, h, pl.ds(64, 64), :] = t[d, h]
            u[d, h, pl.ds(128, 64), :] = after(value).astype(BF16)
    total = None
    for i in range(9):
        parts = [u[i // 3, i % 3 + j] for j in range(2)]
        term = dot(w3[i], jnp.concatenate(parts, 1))
        total = term if total is None else total + term
    total = leaky(total)
    of[pl.ds(0, 128, stride=2), :] = total[:, 0:128]
    of[pl.ds(1, 128, stride=2), :] = total[:, 128:256]
    ob[...] = of[...].astype(BF16)
    store = pltpu.make_async_copy(ob, out, load_sem.at[0])
    store.start()
    sent(g, 4, 8, 3, 0)
    sent(t, 1, 2, 1, 8)
    store.wait()


def shards(depths, heights, volume, first, second, third):
    phases = jnp.asarray(phase_matrix(), BF16)
    placement = jnp.asarray(first_placement(), BF16)
    result = pl.pallas_call(
        functools.partial(body, depths, heights),
        out_shape=pltpu.VMEM((256, 128), BF16),
        in_specs=[pl.BlockSpec(memory_space=pltpu.HBM)] * 6,
        out_specs=pl.BlockSpec(memory_space=pltpu.VMEM),
        scratch_shapes=[
            pltpu.VMEM((4, 4, 8, 512), BF16),
            pltpu.VMEM((3, 3, 3, 4, 32), BF16),
            pltpu.VMEM((3, 3, 96, 64), BF16),
            pltpu.VMEM((3, 3, 192, 128), BF16),
            pltpu.VMEM((512, 512), BF16),
            pltpu.VMEM((128, 4096), BF16),
            pltpu.VMEM((512, 128), F32),
            pltpu.VMEM((10, 14, 16, 128), BF16),
            pltpu.VMEM((10, 14, 16, 128), BF16),
            pltpu.VMEM((10, 14, 16, 128), BF16),
            pltpu.VMEM((128, 32), F32),
            pltpu.VMEM((2, 256, 256), BF16),
            pltpu.VMEM((4, 6, 128, 128), BF16),
            pltpu.VMEM((256, 1536), BF16),
            pltpu.VMEM((3, 4, 64, 128), BF16),
            pltpu.VMEM((3, 4, 192, 128), BF16),
            pltpu.VMEM((9, 128, 192), BF16),
            pltpu.VMEM((256, 128), F32),
            pltpu.VMEM((256, 128), BF16),
            pltpu.SemaphoreType.DMA((6,)),
            pltpu.SemaphoreType.DMA((16,)),
            pltpu.SemaphoreType.DMA((16,)),
        ],
        compiler_params=pltpu.CompilerParams(
            collective_id=0, has_side_effects=True
        ),
        cost_estimate=pl.CostEstimate(flops=2 * 10**9, bytes_accessed=3 * 10**6, transcendentals=0),
        name="layers",
    )(volume, first, second.reshape(3, 3, 96, 64), third.reshape(3, 3, 192, 128), phases, placement)
    return result.reshape(128, 1, 2, 128)


def solution(mesh):
    in_specs = (P(None, "depth", "height", None), P(), P(), P())
    out_specs = P(None, "depth", "height", None)
    local = functools.partial(shards, mesh.shape["depth"], mesh.shape["height"])
    return jax.shard_map(local, mesh=mesh, in_specs=in_specs, out_specs=out_specs, check_vma=False)
```

```python
import functools

import jax
import jax.numpy as jnp
import numpy as np
from jax import lax
from jax.experimental import pallas as pl
from jax.experimental.pallas import tpu as pltpu
from jax.sharding import PartitionSpec as P

MESH = pl.DeviceIdType.MESH
BF16 = jnp.bfloat16
F32 = jnp.float32
SLOPE = 0.3
SIDES = [(a, b) for b in (-1, 1, 0) for a in (0, -1, 1) if (a, b) != (0, 0)]


def phase_matrix():
    cell = lax.broadcasted_iota(jnp.int32, (512, 512), 0)
    column = lax.broadcasted_iota(jnp.int32, (512, 512), 1)
    return jnp.where(cell == 4 * (column & 127) + (column >> 7), 1.0, 0.0).astype(BF16)


def first_placement():
    place = np.zeros((3, 3, 3, 4, 2, 2, 2, 2, 4, 4, 4, 4), np.float32)
    order = ((1, 2, 3, 0), (3, 0, 1, 2))
    for a, b, e, c, s, pd, ph, pw in np.ndindex(3, 3, 3, 4, 2, 2, 2, 2):
        place[a, b, e, c, s, pd, ph, pw, pd + a, ph + b, order[s].index(pw + e), c] = 1
    return np.pad(place.reshape(108, 4096), ((0, 20), (0, 0)))


def nt_dot(left, right):
    return lax.dot_general(left, right, (((1,), (1,)), ((), ())), preferred_element_type=F32)


def dot(left, right):
    return jnp.dot(left, right, preferred_element_type=F32)


def eye(size):
    rows = lax.broadcasted_iota(jnp.int32, (size, size), 0)
    columns = lax.broadcasted_iota(jnp.int32, (size, size), 1)
    return jnp.where(rows == columns, 1.0, 0.0).astype(BF16)


def before(value):
    lane = lax.broadcasted_iota(jnp.int32, value.shape, 1)
    return jnp.where(lane == 0, jnp.zeros_like(value), pltpu.roll(value, 1, 1))


def after(value):
    lane = lax.broadcasted_iota(jnp.int32, value.shape, 1)
    return jnp.where(lane == 127, jnp.zeros_like(value), pltpu.roll(value, 127, 1))


def leaky(value):
    return jnp.where(value > 0, value, SLOPE * value)


def span(shift, size, halo, received):
    if shift == 0:
        return pl.ds(halo, size)
    if received:
        return pl.ds(0, halo) if shift == 1 else pl.ds(halo + size, halo)
    return pl.ds(size, halo) if shift == 1 else pl.ds(halo, halo)


def body(
    depths, heights,
    volume, first, second, third, placement, out,
    x, k1, k2, k3, place, y, g, e0, e1, k1f, w1, f, w2, t, u, w3, acc, of,
    load_sem, send_sem, recv_sem,
):
    di, hi = lax.axis_index("depth"), lax.axis_index("height")

    def within(a, b):
        return (di + a >= 0) & (di + a < depths) & (hi + b >= 0) & (hi + b < heights)

    barrier = pltpu.get_barrier_semaphore()
    for a, b in SIDES:
        @pl.when(within(a, b))
        def _():
            pl.semaphore_signal(barrier, inc=1, device_id=(di + a, hi + b), device_id_type=MESH)

    loads = [
        pltpu.make_async_copy(source, target, load_sem.at[i])
        for i, (source, target) in enumerate(
            ((volume, x), (first, k1), (placement, place), (second, k2), (third, k3))
        )
    ]
    for load in loads:
        load.start()

    for a, b in SIDES:
        @pl.when(jnp.logical_not(within(-a, -b)))
        def _():
            d1, h1 = span(a, 4, 3, True), span(b, 8, 3, True)
            g[d1, h1] = jnp.zeros((d1.size, h1.size, 16, 128), BF16)
            d2, h2 = span(a, 1, 1, True), span(b, 2, 1, True)
            t[d2, h2] = jnp.zeros((d2.size, h2.size, 64, 128), BF16)

    phase = phase_matrix()
    loads[0].wait()
    spread = dot(x[...].reshape(128, 512), phase)
    for i in range(4):
        y[pl.ds(i * 128, 128), :] = spread[:, i * 128 : (i + 1) * 128]
    for d in range(4):
        for h in range(8):
            g[3 + d, 3 + h] = y[pl.ds(d * 8 + h, 16, stride=32), :].astype(BF16)

    count_d = 1 + (di > 0).astype(jnp.int32) + (di < depths - 1).astype(jnp.int32)
    count_h = 1 + (hi > 0).astype(jnp.int32) + (hi < heights - 1).astype(jnp.int32)
    pl.semaphore_wait(barrier, count_d * count_h - 1)

    halo = []
    for i, (a, b) in enumerate(SIDES):
        copy = pltpu.make_async_remote_copy(
            src_ref=g.at[span(a, 4, 3, False), span(b, 8, 3, False)],
            dst_ref=g.at[span(a, 4, 3, True), span(b, 8, 3, True)],
            send_sem=send_sem.at[i],
            recv_sem=recv_sem.at[i],
            device_id=(di + a, hi + b),
            device_id_type=MESH,
        )
        pl.when(within(a, b))(copy.start)
        halo.append(((a, b), copy))

    def arrive(shift):
        for (a, b), copy in halo:
            if b == shift:
                pl.when(within(-a, -b))(copy.wait_recv)

    def row_copy(r, a, b, index):
        return pltpu.make_async_remote_copy(
            src_ref=t.at[1, 1 + r],
            dst_ref=t.at[1 - a, 1 + r if b is None else 3 - 3 * r],
            send_sem=send_sem.at[8 + 5 * r + index],
            recv_sem=recv_sem.at[8 + 5 * r + index],
            device_id=(di + a, hi if b is None else hi + b),
            device_id_type=MESH,
        )

    def row_copies(r):
        b = 2 * r - 1
        side = [(a, b, row_copy(r, a, b, 2 + i)) for i, a in enumerate((0, -1, 1))]
        return side + [(a, 0, row_copy(r, a, None, i)) for i, a in enumerate((-1, 1))]

    for load in loads[1:]:
        load.wait()
    k1f[...] = jnp.zeros_like(k1f)
    for i, (a, b, e) in enumerate(np.ndindex(3, 3, 3)):
        k1f[pl.ds(4 * i, 4), :] = k1[a, b, e].astype(F32)
    flat = nt_dot(eye(32), k1f[...].astype(BF16)).astype(BF16)
    for s in range(2):
        for p in range(0, 8, 4):
            wide = dot(flat, place[:, pl.ds((s * 8 + p) * 256, 1024)]).astype(BF16)
            for q in range(4):
                w1[s, pl.ds((p + q) * 32, 32), :] = wide[:, q * 256 : (q + 1) * 256]

    unit = eye(64)
    blank = jnp.zeros((32, 64), BF16)
    for a in range(3):
        for b in range(3):
            taps = k2[a, b].reshape(96, 64)
            turned = nt_dot(unit, jnp.concatenate([taps, blank, blank, taps], 0)).astype(BF16)
            for ph in range(2):
                for pw in range(2):
                    w2[pl.ds(ph * 128 + pw * 64, 64), pl.ds((a * 4 + b + ph) * 128, 128)] = turned[
                        :, pw * 128 : (pw + 1) * 128
                    ]
        for ph, h in ((0, 3), (1, 0)):
            w2[pl.ds(ph * 128, 128), pl.ds((a * 4 + h) * 128, 128)] = jnp.zeros((128, 128), BF16)

    unit = eye(128)
    for i in range(9):
        rows = k3[i // 3, i % 3].reshape(192, 128)
        w3[i] = nt_dot(unit, rows).astype(BF16)

    def widen(d0, depth, h0, height):
        here = pl.ds(d0, depth), pl.ds(h0, height)
        value = g[here].reshape(depth * height * 16, 128)
        row = lax.broadcasted_iota(jnp.int32, value.shape, 0) & 15
        shape = (depth, height, 16, 128)
        e0[here] = jnp.where(row >= 12, before(value), value).reshape(shape)
        e1[here] = jnp.where(row < 4, after(value), value).reshape(shape)

    def first_layer(hp):
        for dp in range(4):
            deep = 2 * di + dp - 1
            deep_in = (deep >= 0) & (deep < 2 * depths)
            halves = []
            for s, e in enumerate((e0, e1)):
                parts = [
                    e[pl.ds(2 * dp, 4), pl.ds(2 * (hp + j), 4)].reshape(256, 128) for j in range(2)
                ]
                sums = dot(w1[s], jnp.concatenate(parts, 1))
                halves.append(leaky(jnp.max(sums.reshape(8, 32, 256), axis=0)))
            for j in range(2):
                tall = 4 * hi + hp + j - 1
                keep = jnp.where(deep_in & (tall >= 0) & (tall < 4 * heights), 1.0, 0.0)
                p0, p1 = ((half[:, j * 128 : (j + 1) * 128] * keep).astype(BF16) for half in halves)
                for i, part in enumerate((before(p1), p0, p1, after(p0))):
                    f[dp, hp + j, pl.ds(32 * i, 32), :] = part

    widen(3, 4, 3, 8)
    arrive(0)
    widen(0, 3, 3, 8)
    widen(7, 3, 3, 8)
    first_layer(2)

    turn = ((hi & 7) == 0).astype(jnp.int32)

    @pl.loop(0, 2)
    def _(k):
        r = k + turn * (1 - 2 * k)
        pl.when(r == 0)(lambda: arrive(1))
        pl.when(r == 1)(lambda: arrive(-1))
        widen(0, 10, 11 * r, 3)
        first_layer(4 * r)
        parts = [f[pl.ds(pd, 3), pl.ds(2 * r, 4)].reshape(1536, 128) for pd in range(2)]
        sums = dot(w2[...], jnp.concatenate(parts, 1))
        sums = jnp.max(sums.reshape(4, 64, 256), axis=0)
        t[1, 1 + r] = leaky(jnp.maximum(sums[:, 0:128], sums[:, 128:256])).astype(BF16)
        for a, b, copy in row_copies(r):
            pl.when(within(a, b))(copy.start)

    def spread_taps(d, h):
        value = t[d, h]
        u[d, h, pl.ds(0, 64), :] = before(value)
        u[d, h, pl.ds(64, 64), :] = value
        u[d, h, pl.ds(128, 64), :] = after(value)

    spread_taps(1, 1)
    spread_taps(1, 2)
    for r in range(2):
        for a, b, copy in row_copies(r)[3:]:
            pl.when(within(-a, 0))(copy.wait_recv)
    for d in (0, 2):
        for h in (1, 2):
            spread_taps(d, h)
    totals = [None, None]
    for d in range(3):
        both = dot(w3[3 * d + 1], jnp.concatenate([u[d, 1], u[d, 2]], 1))
        terms = both[:, 0:128] + dot(w3[3 * d + 2], u[d, 2]), both[:, 128:256] + dot(w3[3 * d], u[d, 1])
        totals = [term if total is None else total + term for total, term in zip(totals, terms)]
    for j in range(2):
        acc[j] = totals[j]

    @pl.loop(0, 2)
    def _(k):
        side = k + turn * (1 - 2 * k)
        for a, b, copy in row_copies(1 - side)[:3]:
            pl.when(within(-a, -b))(copy.wait_recv)
        total = acc[side]
        for d in range(3):
            spread_taps(d, 3 * side)
            total = total + dot(w3[3 * d + 2 * side], u[d, 3 * side])
        of[pl.ds(side, 128, stride=2), :] = leaky(total)

    out[...] = of[...].astype(BF16)
    for (a, b), copy in halo:
        pl.when(within(a, b))(copy.wait_send)
    for r in range(2):
        for a, b, copy in row_copies(r):
            pl.when(within(a, b))(copy.wait_send)


def shards(depths, heights, volume, first, second, third):
    placement = jnp.asarray(first_placement(), BF16)
    result = pl.pallas_call(
        functools.partial(body, depths, heights),
        out_shape=pltpu.VMEM((256, 128), BF16),
        in_specs=[pl.BlockSpec(memory_space=pltpu.HBM)] * 5,
        out_specs=pl.BlockSpec(memory_space=pltpu.VMEM),
        scratch_shapes=[
            pltpu.VMEM((4, 4, 8, 512), BF16),
            pltpu.VMEM((3, 3, 3, 4, 32), BF16),
            pltpu.VMEM((3, 3, 96, 64), BF16),
            pltpu.VMEM((3, 3, 192, 128), BF16),
            pltpu.VMEM((128, 4096), BF16),
            pltpu.VMEM((512, 128), F32),
            pltpu.VMEM((10, 14, 16, 128), BF16),
            pltpu.VMEM((10, 14, 16, 128), BF16),
            pltpu.VMEM((10, 14, 16, 128), BF16),
            pltpu.VMEM((128, 32), F32),
            pltpu.VMEM((2, 256, 256), BF16),
            pltpu.VMEM((4, 6, 128, 128), BF16),
            pltpu.VMEM((256, 1536), BF16),
            pltpu.VMEM((3, 4, 64, 128), BF16),
            pltpu.VMEM((3, 4, 192, 128), BF16),
            pltpu.VMEM((9, 128, 192), BF16),
            pltpu.VMEM((2, 128, 128), F32),
            pltpu.VMEM((256, 128), F32),
            pltpu.SemaphoreType.DMA((5,)),
            pltpu.SemaphoreType.DMA((18,)),
            pltpu.SemaphoreType.DMA((18,)),
        ],
        compiler_params=pltpu.CompilerParams(
            collective_id=0, has_side_effects=True
        ),
        cost_estimate=pl.CostEstimate(flops=2 * 10**9, bytes_accessed=3 * 10**6, transcendentals=0),
        name="layers",
    )(volume, first, second.reshape(3, 3, 96, 64), third.reshape(3, 3, 192, 128), placement)
    return result.reshape(128, 1, 2, 128)


def solution(mesh):
    in_specs = (P(None, "depth", "height", None), P(), P(), P())
    out_specs = P(None, "depth", "height", None)
    local = functools.partial(shards, mesh.shape["depth"], mesh.shape["height"])
    return jax.shard_map(local, mesh=mesh, in_specs=in_specs, out_specs=out_specs, check_vma=False)
```

```python
import functools

import jax
import jax.numpy as jnp
import numpy as np
from jax import lax
from jax.experimental import pallas as pl
from jax.experimental.pallas import tpu as pltpu
from jax.sharding import PartitionSpec as P

MESH = pl.DeviceIdType.MESH
BF16 = jnp.bfloat16
F32 = jnp.float32
SLOPE = 0.3
RING = 8
SIDES = [(a, b) for b in (1, -1, 0) for a in (0, -1, 1) if (a, b) != (0, 0)]


def phase_matrix():
    cell = lax.broadcasted_iota(jnp.int32, (512, 512), 0)
    column = lax.broadcasted_iota(jnp.int32, (512, 512), 1)
    return jnp.where(cell == 4 * (column & 127) + (column >> 7), 1.0, 0.0).astype(BF16)


def first_placement():
    place = np.zeros((3, 3, 3, 4, 2, 2, 2, 2, 4, 4, 4, 4), np.float32)
    order = ((1, 2, 3, 0), (3, 0, 1, 2))
    for a, b, e, c, s, pd, ph, pw in np.ndindex(3, 3, 3, 4, 2, 2, 2, 2):
        place[a, b, e, c, s, pd, ph, pw, pd + a, ph + b, order[s].index(pw + e), c] = 1
    return np.pad(place.reshape(108, 4096), ((0, 20), (0, 0)))


def nt_dot(left, right):
    return lax.dot_general(left, right, (((1,), (1,)), ((), ())), preferred_element_type=F32)


def dot(left, right):
    return jnp.dot(left, right, preferred_element_type=F32)


def eye(size):
    rows = lax.broadcasted_iota(jnp.int32, (size, size), 0)
    columns = lax.broadcasted_iota(jnp.int32, (size, size), 1)
    return jnp.where(rows == columns, 1.0, 0.0).astype(BF16)


def before(value):
    lane = lax.broadcasted_iota(jnp.int32, value.shape, 1)
    return jnp.where(lane == 0, jnp.zeros_like(value), pltpu.roll(value, 1, 1))


def after(value):
    lane = lax.broadcasted_iota(jnp.int32, value.shape, 1)
    return jnp.where(lane == 127, jnp.zeros_like(value), pltpu.roll(value, 127, 1))


def leaky(value):
    return jnp.where(value > 0, value, SLOPE * value)


def span(shift, size, halo, received):
    if shift == 0:
        return pl.ds(halo, size)
    if received:
        return pl.ds(0, halo) if shift == 1 else pl.ds(halo + size, halo)
    return pl.ds(size, halo) if shift == 1 else pl.ds(halo, halo)


def body(
    depths, heights,
    volume, first, second, third, placement, out,
    x, k1, k2, k3, place, y, g, e0, e1, k1f, w1, f, w2, half, t, u, w3, acc, of,
    passed, load_sem, send_sem, recv_sem, door,
):
    di, hi = lax.axis_index("depth"), lax.axis_index("height")

    def within(a, b):
        return (di + a >= 0) & (di + a < depths) & (hi + b >= 0) & (hi + b < heights)

    loads = [
        pltpu.make_async_copy(source, target, load_sem.at[i])
        for i, (source, target) in enumerate(
            ((volume, x), (first, k1), (placement, place), (second, k2), (third, k3))
        )
    ]
    loads[0].start()

    late = (lax.rem(hi, RING) == RING - 1) & (hi + 1 < heights)
    source = (lax.rem(hi, RING) == 0) & (hi > 0)
    relay = (lax.rem(hi, RING) == 0) & (hi + RING < heights)

    barrier = pltpu.get_barrier_semaphore()

    def greet(semaphore, a, b, condition):
        @pl.when(condition & within(a, b))
        def _():
            pl.semaphore_signal(semaphore, inc=1, device_id=(di + a, hi + b), device_id_type=MESH)

    for a, b in SIDES:
        greet(barrier, a, b, jnp.logical_not(late) if b == 1 else True)
    for a in (0, -1, 1):
        greet(barrier, a, RING - 1, relay)
    greet(barrier, 0, RING, relay)
    for load in loads[1:]:
        load.start()

    for a, b in SIDES:
        @pl.when(jnp.logical_not(within(-a, -b)))
        def _():
            d1, h1 = span(a, 4, 3, True), span(b, 8, 3, True)
            g[d1, h1] = jnp.zeros((d1.size, h1.size, 16, 128), BF16)
            d2, h2 = span(a, 1, 1, True), span(b, 2, 1, True)
            t[d2, h2] = jnp.zeros((d2.size, h2.size, 64, 128), BF16)

    phase = phase_matrix()
    loads[0].wait()
    spread = dot(x[...].reshape(128, 512), phase)
    for i in range(4):
        y[pl.ds(i * 128, 128), :] = spread[:, i * 128 : (i + 1) * 128]
    for d in range(4):
        for h in range(8):
            g[3 + d, 3 + h] = y[pl.ds(d * 8 + h, 16, stride=32), :].astype(BF16)

    count_d = 1 + (di > 0).astype(jnp.int32) + (di < depths - 1).astype(jnp.int32)
    count_h = 1 + (hi > 0).astype(jnp.int32) + (hi < heights - 1).astype(jnp.int32)
    more = jnp.where(late, count_d, 0) + jnp.where(source, 1 - count_d, 0)
    pl.semaphore_wait(barrier, count_d * count_h - 1 + more)
    for a in (0, -1, 1):
        greet(door.at[2 - a], a, 1 - RING, late)
    for a in (0, -1, 1):
        greet(door.at[0], a, 1, late)

    passing = pltpu.make_async_remote_copy(
        src_ref=g.at[pl.ds(3, 4), pl.ds(3, 3)],
        dst_ref=passed,
        send_sem=send_sem.at[21],
        recv_sem=recv_sem.at[18],
        device_id=(di, hi - RING),
        device_id_type=MESH,
    )
    pl.when(source)(passing.start)

    halo = []
    for i, (a, b) in enumerate(SIDES):
        copy = pltpu.make_async_remote_copy(
            src_ref=g.at[span(a, 4, 3, False), span(b, 8, 3, False)],
            dst_ref=g.at[span(a, 4, 3, True), span(b, 8, 3, True)],
            send_sem=send_sem.at[i],
            recv_sem=recv_sem.at[i],
            device_id=(di + a, hi + b),
            device_id_type=MESH,
        )
        direct = within(a, b) & jnp.logical_not(source) if b == -1 else within(a, b)
        pl.when(direct)(copy.start)
        halo.append(((a, b), copy, direct))

    relayed = []
    for i, a in enumerate((0, -1, 1)):
        first_plane, planes = (max(a, 0), 4 - abs(a))
        copy = pltpu.make_async_remote_copy(
            src_ref=passed.at[pl.ds(first_plane, planes)],
            dst_ref=g.at[span(a, 4, 3, True), span(-1, 8, 3, True)],
            send_sem=send_sem.at[18 + i],
            recv_sem=recv_sem.at[SIDES.index((a, -1))],
            device_id=(di + a, hi + RING - 1),
            device_id_type=MESH,
        )
        relayed.append((a, copy))

    def arrive(shift):
        for (a, b), copy, direct in halo:
            if b == shift:
                pl.when(within(-a, -b))(copy.wait_recv)

    def row_copy(r, a, b, index):
        return pltpu.make_async_remote_copy(
            src_ref=t.at[1, 1 + r],
            dst_ref=t.at[1 - a, 1 + r if b is None else 3 - 3 * r],
            send_sem=send_sem.at[8 + 5 * r + index],
            recv_sem=recv_sem.at[8 + 5 * r + index],
            device_id=(di + a, hi if b is None else hi + b),
            device_id_type=MESH,
        )

    row_copies = []
    for r in range(2):
        side = [(a, 2 * r - 1, row_copy(r, a, 2 * r - 1, 2 + i)) for i, a in enumerate((0, -1, 1))]
        row_copies.append(side + [(a, 0, row_copy(r, a, None, i)) for i, a in enumerate((-1, 1))])

    for load in loads[1:]:
        load.wait()
    k1f[...] = jnp.zeros_like(k1f)
    for i, (a, b, e) in enumerate(np.ndindex(3, 3, 3)):
        k1f[pl.ds(4 * i, 4), :] = k1[a, b, e].astype(F32)
    flat = nt_dot(eye(32), k1f[...].astype(BF16)).astype(BF16)
    for s in range(2):
        for p in range(0, 8, 4):
            wide = dot(flat, place[:, pl.ds((s * 8 + p) * 256, 1024)]).astype(BF16)
            for q in range(4):
                w1[s, pl.ds((p + q) * 32, 32), :] = wide[:, q * 256 : (q + 1) * 256]

    unit = eye(64)
    blank = jnp.zeros((32, 64), BF16)
    for a in range(3):
        for b in range(3):
            taps = k2[a, b].reshape(96, 64)
            turned = nt_dot(unit, jnp.concatenate([taps, blank, blank, taps], 0)).astype(BF16)
            for ph in range(2):
                for pw in range(2):
                    h = b + ph
                    w2[2 * a + h // 2, pl.ds(ph * 128 + pw * 64, 64), pl.ds(h % 2 * 128, 128)] = turned[
                        :, pw * 128 : (pw + 1) * 128
                    ]
        for ph, h in ((0, 3), (1, 0)):
            w2[2 * a + h // 2, pl.ds(ph * 128, 128), pl.ds(h % 2 * 128, 128)] = jnp.zeros((128, 128), BF16)

    unit = eye(128)
    for i in range(9):
        rows = k3[i // 3, i % 3].reshape(192, 128)
        w3[i] = nt_dot(unit, rows).astype(BF16)

    def widen(d0, depth, h0, height):
        here = pl.ds(d0, depth), pl.ds(h0, height)
        value = g[here].reshape(depth * height * 16, 128)
        row = lax.broadcasted_iota(jnp.int32, value.shape, 0) & 15
        shape = (depth, height, 16, 128)
        e0[here] = jnp.where(row >= 12, before(value), value).reshape(shape)
        e1[here] = jnp.where(row < 4, after(value), value).reshape(shape)

    def first_layer(hp):
        for dp in range(4):
            deep = 2 * di + dp - 1
            deep_in = (deep >= 0) & (deep < 2 * depths)
            halves = []
            for s, e in enumerate((e0, e1)):
                parts = [
                    e[pl.ds(2 * dp, 4), pl.ds(2 * (hp + j), 4)].reshape(256, 128) for j in range(2)
                ]
                sums = dot(w1[s], jnp.concatenate(parts, 1))
                halves.append(leaky(jnp.max(sums.reshape(8, 32, 256), axis=0)))
            for j in range(2):
                tall = 4 * hi + hp + j - 1
                keep = jnp.where(deep_in & (tall >= 0) & (tall < 4 * heights), 1.0, 0.0)
                p0, p1 = ((half[:, j * 128 : (j + 1) * 128] * keep).astype(BF16) for half in halves)
                for i, part in enumerate((before(p1), p0, p1, after(p0))):
                    f[dp, hp + j, pl.ds(32 * i, 32), :] = part

    def second_layer(hp, later):
        total = None
        for a in range(3):
            parts = [f[pd + a, pl.ds(hp, 2)].reshape(256, 128) for pd in range(2)]
            term = dot(w2[2 * a + later], jnp.concatenate(parts, 1))
            total = term if total is None else total + term
        return total

    widen(3, 4, 3, 8)
    arrive(0)
    widen(0, 3, 3, 8)
    widen(7, 3, 3, 8)
    first_layer(2)
    for r in range(2):
        half[r] = second_layer(2, 1 - r)

    def finish_row(r):
        arrive(1 - 2 * r)
        widen(0, 10, 11 * r, 3)
        first_layer(4 * r)
        sums = second_layer(4 * r, r) + half[r]
        sums = jnp.max(sums.reshape(4, 64, 256), axis=0)
        t[1, 1 + r] = leaky(jnp.maximum(sums[:, 0:128], sums[:, 128:256])).astype(BF16)
        if r == 0:
            pl.when(source)(lambda: pl.semaphore_wait(door.at[0], count_d))
        for a, b, copy in row_copies[r]:
            pl.when(within(a, b))(copy.start)

    @pl.when(source | late)
    def _():
        finish_row(1)
        finish_row(0)

    @pl.when(jnp.logical_not(source | late))
    def _():
        finish_row(0)
        finish_row(1)

    @pl.when(relay)
    def _():
        passing.wait_recv()
        for a, copy in relayed:
            @pl.when(within(a, 0))
            def _():
                pl.semaphore_wait(door.at[2 + a], 1)
                copy.start()

    def spread_taps(d, h):
        value = t[d, h]
        u[d, h, pl.ds(0, 64), :] = before(value)
        u[d, h, pl.ds(64, 64), :] = value
        u[d, h, pl.ds(128, 64), :] = after(value)

    spread_taps(1, 1)
    spread_taps(1, 2)
    for r in range(2):
        for a, b, copy in row_copies[r][3:]:
            pl.when(within(-a, 0))(copy.wait_recv)
    for d in (0, 2):
        for h in (1, 2):
            spread_taps(d, h)
    totals = [None, None]
    for d in range(3):
        both = dot(w3[3 * d + 1], jnp.concatenate([u[d, 1], u[d, 2]], 1))
        terms = both[:, 0:128] + dot(w3[3 * d + 2], u[d, 2]), both[:, 128:256] + dot(w3[3 * d], u[d, 1])
        totals = [term if total is None else total + term for total, term in zip(totals, terms)]

    for side in (1, 0):
        for a, b, copy in row_copies[1 - side][:3]:
            pl.when(within(-a, -b))(copy.wait_recv)
        total = totals[side]
        for d in range(3):
            spread_taps(d, 3 * side)
            total = total + dot(w3[3 * d + 2 * side], u[d, 3 * side])
        of[pl.ds(side, 128, stride=2), :] = leaky(total)

    out[...] = of[...].astype(BF16)
    pl.when(source)(passing.wait_send)
    for a, copy in relayed:
        pl.when(relay & within(a, 0))(copy.wait_send)
    for _, copy, direct in halo:
        pl.when(direct)(copy.wait_send)
    for r in range(2):
        for a, b, copy in row_copies[r]:
            pl.when(within(a, b))(copy.wait_send)


def shards(depths, heights, volume, first, second, third):
    placement = jnp.asarray(first_placement(), BF16)
    result = pl.pallas_call(
        functools.partial(body, depths, heights),
        out_shape=pltpu.VMEM((256, 128), BF16),
        in_specs=[pl.BlockSpec(memory_space=pltpu.HBM)] * 5,
        out_specs=pl.BlockSpec(memory_space=pltpu.VMEM),
        scratch_shapes=[
            pltpu.VMEM((4, 4, 8, 512), BF16),
            pltpu.VMEM((3, 3, 3, 4, 32), BF16),
            pltpu.VMEM((3, 3, 96, 64), BF16),
            pltpu.VMEM((3, 3, 192, 128), BF16),
            pltpu.VMEM((128, 4096), BF16),
            pltpu.VMEM((512, 128), F32),
            pltpu.VMEM((10, 14, 16, 128), BF16),
            pltpu.VMEM((10, 14, 16, 128), BF16),
            pltpu.VMEM((10, 14, 16, 128), BF16),
            pltpu.VMEM((128, 32), F32),
            pltpu.VMEM((2, 256, 256), BF16),
            pltpu.VMEM((4, 6, 128, 128), BF16),
            pltpu.VMEM((6, 256, 256), BF16),
            pltpu.VMEM((2, 256, 256), F32),
            pltpu.VMEM((3, 4, 64, 128), BF16),
            pltpu.VMEM((3, 4, 192, 128), BF16),
            pltpu.VMEM((9, 128, 192), BF16),
            pltpu.VMEM((2, 128, 128), F32),
            pltpu.VMEM((256, 128), F32),
            pltpu.VMEM((4, 3, 16, 128), BF16),
            pltpu.SemaphoreType.DMA((5,)),
            pltpu.SemaphoreType.DMA((22,)),
            pltpu.SemaphoreType.DMA((19,)),
            pltpu.SemaphoreType.REGULAR((4,)),
        ],
        compiler_params=pltpu.CompilerParams(
            collective_id=0, has_side_effects=True
        ),
        cost_estimate=pl.CostEstimate(flops=2 * 10**9, bytes_accessed=3 * 10**6, transcendentals=0),
        name="layers",
    )(volume, first, second.reshape(3, 3, 96, 64), third.reshape(3, 3, 192, 128), placement)
    return result.reshape(128, 1, 2, 128)


def solution(mesh):
    in_specs = (P(None, "depth", "height", None), P(), P(), P())
    out_specs = P(None, "depth", "height", None)
    local = functools.partial(shards, mesh.shape["depth"], mesh.shape["height"])
    return jax.shard_map(local, mesh=mesh, in_specs=in_specs, out_specs=out_specs, check_vma=False)
```

```python
import functools

import jax
import jax.numpy as jnp
import numpy as np
from jax import lax
from jax.experimental import pallas as pl
from jax.experimental.pallas import tpu as pltpu
from jax.sharding import PartitionSpec as P

MESH = pl.DeviceIdType.MESH
BF16 = jnp.bfloat16
F32 = jnp.float32
SLOPE = 0.3
RING = 8
SIDES = [(a, b) for b in (0, 1, -1) for a in (0, -1, 1) if (a, b) != (0, 0)]


def phase_matrix():
    cell = lax.broadcasted_iota(jnp.int32, (512, 512), 0)
    column = lax.broadcasted_iota(jnp.int32, (512, 512), 1)
    return jnp.where(cell == 4 * (column & 127) + (column >> 7), 1.0, 0.0).astype(BF16)


def first_placement():
    place = np.zeros((3, 3, 3, 4, 2, 2, 2, 2, 4, 4, 4, 4), np.float32)
    order = ((1, 2, 3, 0), (3, 0, 1, 2))
    for a, b, e, c, s, pd, ph, pw in np.ndindex(3, 3, 3, 4, 2, 2, 2, 2):
        place[a, b, e, c, s, pd, ph, pw, pd + a, ph + b, order[s].index(pw + e), c] = 1
    return np.pad(place.reshape(108, 4096), ((0, 20), (0, 0)))


def nt_dot(left, right):
    return lax.dot_general(left, right, (((1,), (1,)), ((), ())), preferred_element_type=F32)


def dot(left, right):
    return jnp.dot(left, right, preferred_element_type=F32)


def eye(size):
    rows = lax.broadcasted_iota(jnp.int32, (size, size), 0)
    columns = lax.broadcasted_iota(jnp.int32, (size, size), 1)
    return jnp.where(rows == columns, 1.0, 0.0).astype(BF16)


def before(value):
    lane = lax.broadcasted_iota(jnp.int32, value.shape, 1)
    return jnp.where(lane == 0, jnp.zeros_like(value), pltpu.roll(value, 1, 1))


def after(value):
    lane = lax.broadcasted_iota(jnp.int32, value.shape, 1)
    return jnp.where(lane == 127, jnp.zeros_like(value), pltpu.roll(value, 127, 1))


def leaky(value):
    return jnp.where(value > 0, value, SLOPE * value)


def span(shift, size, halo, received):
    if shift == 0:
        return pl.ds(halo, size)
    if received:
        return pl.ds(0, halo) if shift == 1 else pl.ds(halo + size, halo)
    return pl.ds(size, halo) if shift == 1 else pl.ds(halo, halo)


def body(
    depths, heights,
    volume, first, second, third, placement, out,
    x, k1, k2, k3, place, y, g, e0, e1, k1f, w1, f, w2, half, t, u, w3, acc, of,
    passed, load_sem, send_sem, recv_sem, door, go,
):
    di, hi = lax.axis_index("depth"), lax.axis_index("height")

    def within(a, b):
        return (di + a >= 0) & (di + a < depths) & (hi + b >= 0) & (hi + b < heights)

    loads = [
        pltpu.make_async_copy(source, target, load_sem.at[i])
        for i, (source, target) in enumerate(
            ((volume, x), (first, k1), (placement, place), (second, k2), (third, k3))
        )
    ]
    loads[0].start()

    rings = heights == 2 * RING
    late, source = (hi == RING - 1) & rings, (hi == RING) & rings
    relay, herald = (hi == 0) & rings, (hi == 1) & rings

    barrier = pltpu.get_barrier_semaphore()

    def greet(semaphore, a, b, condition):
        @pl.when(condition & within(a, b))
        def _():
            pl.semaphore_signal(semaphore, inc=1, device_id=(di + a, hi + b), device_id_type=MESH)

    for a, b in SIDES:
        greet(barrier, a, b, jnp.logical_not({1: late, 0: relay, -1: herald}[b]))
    for a in (0, -1, 1):
        greet(barrier, a, 1 - RING, late)
    greet(barrier, 0, RING, relay)
    for load in loads[1:]:
        load.start()

    for a, b in SIDES:
        @pl.when(jnp.logical_not(within(-a, -b)))
        def _():
            d1, h1 = span(a, 4, 3, True), span(b, 8, 3, True)
            g[d1, h1] = jnp.zeros((d1.size, h1.size, 16, 128), BF16)
            d2, h2 = span(a, 1, 1, True), span(b, 2, 1, True)
            t[d2, h2] = jnp.zeros((d2.size, h2.size, 64, 128), BF16)

    phase = phase_matrix()
    loads[0].wait()
    spread = dot(x[...].reshape(128, 512), phase)
    for i in range(4):
        y[pl.ds(i * 128, 128), :] = spread[:, i * 128 : (i + 1) * 128]
    for d in range(4):
        for h in range(8):
            g[3 + d, 3 + h] = y[pl.ds(d * 8 + h, 16, stride=32), :].astype(BF16)

    count_d = 1 + (di > 0).astype(jnp.int32) + (di < depths - 1).astype(jnp.int32)
    count_h = 1 + (hi > 0).astype(jnp.int32) + (hi < heights - 1).astype(jnp.int32)
    around = count_d * count_h - 1 + jnp.where(source, 1 - count_d, 0)
    pl.when(jnp.logical_not(relay))(lambda: pl.semaphore_wait(barrier, around))
    greet(go, 0, -1, herald)
    for a in (0, -1, 1):
        greet(door, a, 1, late)
    pl.when(relay)(lambda: pl.semaphore_wait(go, 1))

    passing = pltpu.make_async_remote_copy(
        src_ref=g.at[pl.ds(3, 4), pl.ds(3, 3)],
        dst_ref=passed,
        send_sem=send_sem.at[21],
        recv_sem=recv_sem.at[18],
        device_id=(di, hi - RING),
        device_id_type=MESH,
    )
    pl.when(source)(passing.start)

    relayed = []
    for i, a in enumerate((0, -1, 1)):
        first_plane, planes = (max(a, 0), 4 - abs(a))
        copy = pltpu.make_async_remote_copy(
            src_ref=passed.at[pl.ds(first_plane, planes)],
            dst_ref=g.at[span(a, 4, 3, True), span(-1, 8, 3, True)],
            send_sem=send_sem.at[18 + i],
            recv_sem=recv_sem.at[SIDES.index((a, -1))],
            device_id=(di + a, hi + RING - 1),
            device_id_type=MESH,
        )
        relayed.append((a, copy))

    halo = []
    for i, (a, b) in enumerate(SIDES):
        copy = pltpu.make_async_remote_copy(
            src_ref=g.at[span(a, 4, 3, False), span(b, 8, 3, False)],
            dst_ref=g.at[span(a, 4, 3, True), span(b, 8, 3, True)],
            send_sem=send_sem.at[i],
            recv_sem=recv_sem.at[i],
            device_id=(di + a, hi + b),
            device_id_type=MESH,
        )
        direct = within(a, b) & jnp.logical_not(source) if b == -1 else within(a, b)
        pl.when(direct)(copy.start)
        halo.append(((a, b), copy, direct))

    def arrive(shift):
        for (a, b), copy, direct in halo:
            if b == shift:
                pl.when(within(-a, -b))(copy.wait_recv)

    def row_copy(r, a, b, index):
        return pltpu.make_async_remote_copy(
            src_ref=t.at[1, 1 + r],
            dst_ref=t.at[1 - a, 1 + r if b is None else 3 - 3 * r],
            send_sem=send_sem.at[8 + 5 * r + index],
            recv_sem=recv_sem.at[8 + 5 * r + index],
            device_id=(di + a, hi if b is None else hi + b),
            device_id_type=MESH,
        )

    row_copies = []
    for r in range(2):
        side = [(a, 2 * r - 1, row_copy(r, a, 2 * r - 1, 2 + i)) for i, a in enumerate((0, -1, 1))]
        row_copies.append(side + [(a, 0, row_copy(r, a, None, i)) for i, a in enumerate((-1, 1))])

    for load in loads[1:]:
        load.wait()
    k1f[...] = jnp.zeros_like(k1f)
    for i, (a, b, e) in enumerate(np.ndindex(3, 3, 3)):
        k1f[pl.ds(4 * i, 4), :] = k1[a, b, e].astype(F32)
    flat = nt_dot(eye(32), k1f[...].astype(BF16)).astype(BF16)
    for s in range(2):
        for p in range(0, 8, 4):
            wide = dot(flat, place[:, pl.ds((s * 8 + p) * 256, 1024)]).astype(BF16)
            for q in range(4):
                w1[s, pl.ds((p + q) * 32, 32), :] = wide[:, q * 256 : (q + 1) * 256]

    unit = eye(64)
    blank = jnp.zeros((32, 64), BF16)
    for a in range(3):
        for b in range(3):
            taps = k2[a, b].reshape(96, 64)
            turned = nt_dot(unit, jnp.concatenate([taps, blank, blank, taps], 0)).astype(BF16)
            for ph in range(2):
                for pw in range(2):
                    h = b + ph
                    w2[2 * a + h // 2, pl.ds(ph * 128 + pw * 64, 64), pl.ds(h % 2 * 128, 128)] = turned[
                        :, pw * 128 : (pw + 1) * 128
                    ]
        for ph, h in ((0, 3), (1, 0)):
            w2[2 * a + h // 2, pl.ds(ph * 128, 128), pl.ds(h % 2 * 128, 128)] = jnp.zeros((128, 128), BF16)

    unit = eye(128)
    for i in range(9):
        rows = k3[i // 3, i % 3].reshape(192, 128)
        w3[i] = nt_dot(unit, rows).astype(BF16)

    def widen(d0, depth, h0, height):
        here = pl.ds(d0, depth), pl.ds(h0, height)
        value = g[here].reshape(depth * height * 16, 128)
        row = lax.broadcasted_iota(jnp.int32, value.shape, 0) & 15
        shape = (depth, height, 16, 128)
        e0[here] = jnp.where(row >= 12, before(value), value).reshape(shape)
        e1[here] = jnp.where(row < 4, after(value), value).reshape(shape)

    def first_layer(hp):
        for dp in range(4):
            deep = 2 * di + dp - 1
            deep_in = (deep >= 0) & (deep < 2 * depths)
            halves = []
            for s, e in enumerate((e0, e1)):
                parts = [
                    e[pl.ds(2 * dp, 4), pl.ds(2 * (hp + j), 4)].reshape(256, 128) for j in range(2)
                ]
                sums = dot(w1[s], jnp.concatenate(parts, 1))
                halves.append(leaky(jnp.max(sums.reshape(8, 32, 256), axis=0)))
            for j in range(2):
                tall = 4 * hi + hp + j - 1
                keep = jnp.where(deep_in & (tall >= 0) & (tall < 4 * heights), 1.0, 0.0)
                p0, p1 = ((half[:, j * 128 : (j + 1) * 128] * keep).astype(BF16) for half in halves)
                for i, part in enumerate((before(p1), p0, p1, after(p0))):
                    f[dp, hp + j, pl.ds(32 * i, 32), :] = part

    def second_layer(hp, later):
        total = None
        for a in range(3):
            parts = [f[pd + a, pl.ds(hp, 2)].reshape(256, 128) for pd in range(2)]
            term = dot(w2[2 * a + later], jnp.concatenate(parts, 1))
            total = term if total is None else total + term
        return total

    @pl.when(relay)
    def _():
        pl.semaphore_wait(barrier, count_d)
        passing.wait_recv()
        for a, copy in relayed:
            pl.when(within(a, 0))(copy.start)

    widen(3, 4, 3, 8)
    arrive(0)
    widen(0, 3, 3, 8)
    widen(7, 3, 3, 8)
    first_layer(2)
    for r in range(2):
        half[r] = second_layer(2, 1 - r)

    def finish_row(r):
        arrive(1 - 2 * r)
        widen(0, 10, 11 * r, 3)
        first_layer(4 * r)
        sums = second_layer(4 * r, r) + half[r]
        sums = jnp.max(sums.reshape(4, 64, 256), axis=0)
        t[1, 1 + r] = leaky(jnp.maximum(sums[:, 0:128], sums[:, 128:256])).astype(BF16)
        if r == 0:
            pl.when(source)(lambda: pl.semaphore_wait(door, count_d))
        for a, b, copy in row_copies[r]:
            pl.when(within(a, b))(copy.start)

    @pl.when(source | late)
    def _():
        finish_row(1)
        finish_row(0)

    @pl.when(jnp.logical_not(source | late))
    def _():
        finish_row(0)
        finish_row(1)

    def spread_taps(d, h):
        value = t[d, h]
        u[d, h, pl.ds(0, 64), :] = before(value)
        u[d, h, pl.ds(64, 64), :] = value
        u[d, h, pl.ds(128, 64), :] = after(value)

    spread_taps(1, 1)
    spread_taps(1, 2)
    for r in range(2):
        for a, b, copy in row_copies[r][3:]:
            pl.when(within(-a, 0))(copy.wait_recv)
    for d in (0, 2):
        for h in (1, 2):
            spread_taps(d, h)
    totals = [None, None]
    for d in range(3):
        both = dot(w3[3 * d + 1], jnp.concatenate([u[d, 1], u[d, 2]], 1))
        terms = both[:, 0:128] + dot(w3[3 * d + 2], u[d, 2]), both[:, 128:256] + dot(w3[3 * d], u[d, 1])
        totals = [term if total is None else total + term for total, term in zip(totals, terms)]

    for side in (1, 0):
        for a, b, copy in row_copies[1 - side][:3]:
            pl.when(within(-a, -b))(copy.wait_recv)
        total = totals[side]
        for d in range(3):
            spread_taps(d, 3 * side)
            total = total + dot(w3[3 * d + 2 * side], u[d, 3 * side])
        of[pl.ds(side, 128, stride=2), :] = leaky(total)

    out[...] = of[...].astype(BF16)
    pl.when(source)(passing.wait_send)
    for a, copy in relayed:
        pl.when(relay & within(a, 0))(copy.wait_send)
    for _, copy, direct in halo:
        pl.when(direct)(copy.wait_send)
    for r in range(2):
        for a, b, copy in row_copies[r]:
            pl.when(within(a, b))(copy.wait_send)


def shards(depths, heights, volume, first, second, third):
    placement = jnp.asarray(first_placement(), BF16)
    result = pl.pallas_call(
        functools.partial(body, depths, heights),
        out_shape=pltpu.VMEM((256, 128), BF16),
        in_specs=[pl.BlockSpec(memory_space=pltpu.HBM)] * 5,
        out_specs=pl.BlockSpec(memory_space=pltpu.VMEM),
        scratch_shapes=[
            pltpu.VMEM((4, 4, 8, 512), BF16),
            pltpu.VMEM((3, 3, 3, 4, 32), BF16),
            pltpu.VMEM((3, 3, 96, 64), BF16),
            pltpu.VMEM((3, 3, 192, 128), BF16),
            pltpu.VMEM((128, 4096), BF16),
            pltpu.VMEM((512, 128), F32),
            pltpu.VMEM((10, 14, 16, 128), BF16),
            pltpu.VMEM((10, 14, 16, 128), BF16),
            pltpu.VMEM((10, 14, 16, 128), BF16),
            pltpu.VMEM((128, 32), F32),
            pltpu.VMEM((2, 256, 256), BF16),
            pltpu.VMEM((4, 6, 128, 128), BF16),
            pltpu.VMEM((6, 256, 256), BF16),
            pltpu.VMEM((2, 256, 256), F32),
            pltpu.VMEM((3, 4, 64, 128), BF16),
            pltpu.VMEM((3, 4, 192, 128), BF16),
            pltpu.VMEM((9, 128, 192), BF16),
            pltpu.VMEM((2, 128, 128), F32),
            pltpu.VMEM((256, 128), F32),
            pltpu.VMEM((4, 3, 16, 128), BF16),
            pltpu.SemaphoreType.DMA((5,)),
            pltpu.SemaphoreType.DMA((22,)),
            pltpu.SemaphoreType.DMA((19,)),
            pltpu.SemaphoreType.REGULAR,
            pltpu.SemaphoreType.REGULAR,
        ],
        compiler_params=pltpu.CompilerParams(
            collective_id=0, has_side_effects=True
        ),
        cost_estimate=pl.CostEstimate(flops=2 * 10**9, bytes_accessed=3 * 10**6, transcendentals=0),
        name="layers",
    )(volume, first, second.reshape(3, 3, 96, 64), third.reshape(3, 3, 192, 128), placement)
    return result.reshape(128, 1, 2, 128)


def solution(mesh):
    in_specs = (P(None, "depth", "height", None), P(), P(), P())
    out_specs = P(None, "depth", "height", None)
    local = functools.partial(shards, mesh.shape["depth"], mesh.shape["height"])
    return jax.shard_map(local, mesh=mesh, in_specs=in_specs, out_specs=out_specs, check_vma=False)
```

```python
import functools

import jax
import jax.numpy as jnp
import numpy as np
from jax import lax
from jax.experimental import pallas as pl
from jax.experimental.pallas import tpu as pltpu
from jax.sharding import PartitionSpec as P

MESH = pl.DeviceIdType.MESH
BF16 = jnp.bfloat16
F32 = jnp.float32
SLOPE = 0.3
RING = 8
SIDES = [(a, b) for b in (0, 1, -1) for a in (0, -1, 1) if (a, b) != (0, 0)]


def phase_matrix():
    cell = lax.broadcasted_iota(jnp.int32, (512, 512), 0)
    column = lax.broadcasted_iota(jnp.int32, (512, 512), 1)
    return jnp.where(cell == 4 * (column & 127) + (column >> 7), 1.0, 0.0).astype(BF16)


def first_placement():
    place = np.zeros((3, 3, 3, 4, 2, 2, 2, 2, 4, 4, 4, 4), np.float32)
    order = ((1, 2, 3, 0), (3, 0, 1, 2))
    for a, b, e, c, s, pd, ph, pw in np.ndindex(3, 3, 3, 4, 2, 2, 2, 2):
        place[a, b, e, c, s, pd, ph, pw, pd + a, ph + b, order[s].index(pw + e), c] = 1
    return np.pad(place.reshape(108, 4096), ((0, 20), (0, 0)))


def nt_dot(left, right):
    return lax.dot_general(left, right, (((1,), (1,)), ((), ())), preferred_element_type=F32)


def dot(left, right):
    return jnp.dot(left, right, preferred_element_type=F32)


def eye(size):
    rows = lax.broadcasted_iota(jnp.int32, (size, size), 0)
    columns = lax.broadcasted_iota(jnp.int32, (size, size), 1)
    return jnp.where(rows == columns, 1.0, 0.0).astype(BF16)


def before(value):
    lane = lax.broadcasted_iota(jnp.int32, value.shape, 1)
    return jnp.where(lane == 0, jnp.zeros_like(value), pltpu.roll(value, 1, 1))


def after(value):
    lane = lax.broadcasted_iota(jnp.int32, value.shape, 1)
    return jnp.where(lane == 127, jnp.zeros_like(value), pltpu.roll(value, 127, 1))


def leaky(value):
    return jnp.where(value > 0, value, SLOPE * value)


def span(shift, size, halo, received):
    if shift == 0:
        return pl.ds(halo, size)
    if received:
        return pl.ds(0, halo) if shift == 1 else pl.ds(halo + size, halo)
    return pl.ds(size, halo) if shift == 1 else pl.ds(halo, halo)


def body(
    depths, heights,
    volume, first, second, third, placement, out,
    x, k1, k2, k3, place, y, g, e0, e1, k1f, w1, f, w2, t, u, w3, of,
    passed, load_sem, send_sem, recv_sem, door, go, ready,
):
    di, hi = lax.axis_index("depth"), lax.axis_index("height")

    def within(a, b):
        return (di + a >= 0) & (di + a < depths) & (hi + b >= 0) & (hi + b < heights)

    loads = [
        pltpu.make_async_copy(source, target, load_sem.at[i])
        for i, (source, target) in enumerate(
            ((volume, x), (first, k1), (placement, place), (second, k2), (third, k3))
        )
    ]
    loads[0].start()

    rings = heights == 2 * RING
    late, source = (hi == RING - 1) & rings, (hi == RING) & rings
    relay, herald = (hi == 0) & rings, (hi == 1) & rings

    barrier = pltpu.get_barrier_semaphore()

    def greet(semaphore, a, b, condition):
        @pl.when(condition & within(a, b))
        def _():
            pl.semaphore_signal(semaphore, inc=1, device_id=(di + a, hi + b), device_id_type=MESH)

    greet(barrier, 0, 1 - RING, late)
    for a, b in SIDES:
        greet(barrier, a, b, jnp.logical_not({1: late, 0: relay, -1: herald}[b]))
    greet(barrier, 0, RING, relay)
    phase = phase_matrix()
    loads[0].wait()
    for load in loads[1:]:
        load.start()
    spread = dot(x[...].reshape(128, 512), phase)
    for i in range(4):
        y[pl.ds(i * 128, 128), :] = spread[:, i * 128 : (i + 1) * 128]
    for d in range(4):
        for h in range(8):
            g[3 + d, 3 + h] = y[pl.ds(d * 8 + h, 16, stride=32), :].astype(BF16)

    count_d = 1 + (di > 0).astype(jnp.int32) + (di < depths - 1).astype(jnp.int32)
    count_h = 1 + (hi > 0).astype(jnp.int32) + (hi < heights - 1).astype(jnp.int32)
    around = count_d * count_h - 1 + jnp.where(source, 1 - count_d, 0)
    pl.when(jnp.logical_not(relay))(lambda: pl.semaphore_wait(barrier, around))
    greet(go, 0, -1, herald)
    for a in (-1, 1):
        greet(ready.at[(1 - a) // 2], a, 0, source)
    for a in (0, -1, 1):
        greet(door, a, 1, late)
    pl.when(relay)(lambda: pl.semaphore_wait(go, 1))

    passing, relayed = [], []
    for i, a in enumerate((0, -1, 1)):
        copy = pltpu.make_async_remote_copy(
            src_ref=g.at[span(a, 4, 3, False), pl.ds(3, 3)],
            dst_ref=passed.at[span(a, 4, 3, True)],
            send_sem=send_sem.at[18 + i],
            recv_sem=recv_sem.at[18 + i],
            device_id=(di + a, hi - RING),
            device_id_type=MESH,
        )
        passing.append((a, copy))
        copy = pltpu.make_async_remote_copy(
            src_ref=passed.at[span(a, 4, 3, True)],
            dst_ref=g.at[span(a, 4, 3, True), pl.ds(11, 3)],
            send_sem=send_sem.at[21 + i],
            recv_sem=recv_sem.at[SIDES.index((a, -1))],
            device_id=(di, hi + RING - 1),
            device_id_type=MESH,
        )
        relayed.append((a, copy))

    pl.when(source)(passing[0][1].start)

    mate = {1: lax.rem(di, 2) == 0, -1: lax.rem(di, 2) == 1}
    shared = []
    for i, a in enumerate((-1, 1)):
        copy = pltpu.make_async_remote_copy(
            src_ref=g.at[span(a, 4, 3, False), pl.ds(0, 3)],
            dst_ref=g.at[span(a, 4, 3, True), pl.ds(0, 3)],
            send_sem=send_sem.at[24 + i],
            recv_sem=recv_sem.at[SIDES.index((a, 1))],
            device_id=(di + a, hi),
            device_id_type=MESH,
        )
        shared.append((source & mate[a], copy))

    halo = []
    for i, (a, b) in enumerate(SIDES):
        copy = pltpu.make_async_remote_copy(
            src_ref=g.at[span(a, 4, 3, False), span(b, 8, 3, False)],
            dst_ref=g.at[span(a, 4, 3, True), span(b, 8, 3, True)],
            send_sem=send_sem.at[i],
            recv_sem=recv_sem.at[i],
            device_id=(di + a, hi + b),
            device_id_type=MESH,
        )
        direct = within(a, b)
        if b == -1:
            direct &= jnp.logical_not(source)
        if b == 1 and a != 0:
            direct &= jnp.logical_not(late & mate[a])
        pl.when(direct)(copy.start)
        halo.append(((a, b), copy, direct))

    for a, copy in passing[1:]:
        @pl.when(source & within(a, 0))
        def _():
            pl.semaphore_wait(ready.at[(1 + a) // 2], 1)
            copy.start()

    def arrive(shift):
        for (a, b), copy, direct in halo:
            if b == shift:
                pl.when(within(-a, -b))(copy.wait_recv)
                if (a, b) == (0, 1):
                    for condition, share in shared:
                        pl.when(condition)(share.start)

    def row_copy(r, a, b, index):
        return pltpu.make_async_remote_copy(
            src_ref=t.at[1, 1 + r],
            dst_ref=t.at[1 - a, 1 + r if b is None else 3 - 3 * r],
            send_sem=send_sem.at[8 + 5 * r + index],
            recv_sem=recv_sem.at[8 + 5 * r + index],
            device_id=(di + a, hi if b is None else hi + b),
            device_id_type=MESH,
        )

    row_copies = []
    for r in range(2):
        side = [(a, 2 * r - 1, row_copy(r, a, 2 * r - 1, 2 + i)) for i, a in enumerate((0, -1, 1))]
        row_copies.append(side + [(a, 0, row_copy(r, a, None, i)) for i, a in enumerate((-1, 1))])

    for a, b in SIDES:
        @pl.when(jnp.logical_not(within(-a, -b)))
        def _():
            d1, h1 = span(a, 4, 3, True), span(b, 8, 3, True)
            g[d1, h1] = jnp.zeros((d1.size, h1.size, 16, 128), BF16)
            d2, h2 = span(a, 1, 1, True), span(b, 2, 1, True)
            t[d2, h2] = jnp.zeros((d2.size, h2.size, 64, 128), BF16)

    for load in loads[1:]:
        load.wait()
    k1f[...] = jnp.zeros_like(k1f)
    for i, (a, b, e) in enumerate(np.ndindex(3, 3, 3)):
        k1f[pl.ds(4 * i, 4), :] = k1[a, b, e].astype(F32)
    flat = nt_dot(eye(32), k1f[...].astype(BF16)).astype(BF16)
    for s in range(2):
        for p in range(0, 8, 4):
            wide = dot(flat, place[:, pl.ds((s * 8 + p) * 256, 1024)]).astype(BF16)
            for q in range(4):
                w1[s, pl.ds((p + q) * 32, 32), :] = wide[:, q * 256 : (q + 1) * 256]

    unit = eye(64)
    blank = jnp.zeros((32, 64), BF16)
    for a in range(3):
        for b in range(3):
            taps = k2[a, b].reshape(96, 64)
            turned = nt_dot(unit, jnp.concatenate([taps, blank, blank, taps], 0)).astype(BF16)
            for ph in range(2):
                for pw in range(2):
                    h = b + ph
                    w2[2 * a + h // 2, pl.ds(ph * 128 + pw * 64, 64), pl.ds(h % 2 * 128, 128)] = turned[
                        :, pw * 128 : (pw + 1) * 128
                    ]
        for ph, h in ((0, 3), (1, 0)):
            w2[2 * a + h // 2, pl.ds(ph * 128, 128), pl.ds(h % 2 * 128, 128)] = jnp.zeros((128, 128), BF16)

    unit = eye(128)
    for i in range(9):
        rows = k3[i // 3, i % 3].reshape(192, 128)
        w3[i] = nt_dot(unit, rows).astype(BF16)

    def widen(d0, depth, h0, height):
        here = pl.ds(d0, depth), pl.ds(h0, height)
        value = g[here].reshape(depth * height * 16, 128)
        row = lax.broadcasted_iota(jnp.int32, value.shape, 0) & 15
        shape = (depth, height, 16, 128)
        e0[here] = jnp.where(row >= 12, before(value), value).reshape(shape)
        e1[here] = jnp.where(row < 4, after(value), value).reshape(shape)

    def first_layer(hp):
        for dp in range(4):
            deep = 2 * di + dp - 1
            deep_in = (deep >= 0) & (deep < 2 * depths)
            halves = []
            for s, e in enumerate((e0, e1)):
                parts = [
                    e[pl.ds(2 * dp, 4), pl.ds(2 * (hp + j), 4)].reshape(256, 128) for j in range(2)
                ]
                sums = dot(w1[s], jnp.concatenate(parts, 1))
                halves.append(leaky(jnp.max(sums.reshape(8, 32, 256), axis=0)))
            for j in range(2):
                tall = 4 * hi + hp + j - 1
                keep = jnp.where(deep_in & (tall >= 0) & (tall < 4 * heights), 1.0, 0.0)
                p0, p1 = ((half[:, j * 128 : (j + 1) * 128] * keep).astype(BF16) for half in halves)
                for i, part in enumerate((before(p1), p0, p1, after(p0))):
                    f[dp, hp + j, pl.ds(32 * i, 32), :] = part

    def second_layer(hp, later):
        total = None
        for a in range(3):
            parts = [f[pd + a, pl.ds(hp, 2)].reshape(256, 128) for pd in range(2)]
            term = dot(w2[2 * a + later], jnp.concatenate(parts, 1))
            total = term if total is None else total + term
        return total

    @pl.when(relay)
    def _():
        pl.semaphore_wait(barrier, 1)
        for (a, arriving), (_, leaving) in zip(passing, relayed):
            @pl.when(within(-a, 0))
            def _():
                arriving.wait_recv()
                leaving.start()

    widen(3, 4, 3, 8)
    arrive(0)
    widen(0, 3, 3, 8)
    widen(7, 3, 3, 8)
    first_layer(2)

    def finish_row(r):
        half = second_layer(2, 1 - r)
        arrive(1 - 2 * r)
        widen(0, 10, 11 * r, 3)
        first_layer(4 * r)
        sums = second_layer(4 * r, r) + half
        sums = jnp.max(sums.reshape(4, 64, 256), axis=0)
        t[1, 1 + r] = leaky(jnp.maximum(sums[:, 0:128], sums[:, 128:256])).astype(BF16)
        if r == 0:
            pl.when(source)(lambda: pl.semaphore_wait(door, count_d))
        for a, b, copy in row_copies[r]:
            pl.when(within(a, b))(copy.start)

    @pl.when(source | late)
    def _():
        finish_row(1)
        finish_row(0)

    @pl.when(jnp.logical_not(source | late))
    def _():
        finish_row(0)
        finish_row(1)

    def spread_taps(d, h):
        value = t[d, h]
        u[d, h, pl.ds(0, 64), :] = before(value)
        u[d, h, pl.ds(64, 64), :] = value
        u[d, h, pl.ds(128, 64), :] = after(value)

    def add_row(h, depths_here):
        for d in depths_here:
            spread_taps(d, h)
            places = [j for j in range(2) if 0 <= h - j <= 2]
            terms = dot(jnp.concatenate([w3[3 * d + h - j] for j in places], 0), u[d, h])
            for i, j in enumerate(places):
                term = terms[i * 128 : (i + 1) * 128]
                totals[j] = term if totals[j] is None else totals[j] + term

    def rows_arrive(r, side):
        for a, b, copy in row_copies[r]:
            if (b != 0) == side:
                pl.when(within(-a, -b))(copy.wait_recv)

    totals = [None, None]
    add_row(1, (1,))
    add_row(2, (1,))
    for condition, copy in shared:
        pl.when(condition)(copy.wait_send)
    for a, copy in passing:
        pl.when(source & within(a, 0))(copy.wait_send)
    for a, copy in relayed:
        pl.when(relay & within(-a, 0))(copy.wait_send)
    for _, copy, direct in halo:
        pl.when(direct)(copy.wait_send)
    rows_arrive(1, False)
    add_row(2, (0, 2))
    rows_arrive(0, True)
    add_row(3, (0, 1, 2))
    rows_arrive(0, False)
    add_row(1, (0, 2))
    of[pl.ds(1, 128, stride=2), :] = leaky(totals[1])
    rows_arrive(1, True)
    add_row(0, (0, 1, 2))
    of[pl.ds(0, 128, stride=2), :] = leaky(totals[0])

    out[...] = of[...].astype(BF16)
    for r in range(2):
        for a, b, copy in row_copies[r]:
            pl.when(within(a, b))(copy.wait_send)


def shards(depths, heights, volume, first, second, third):
    placement = jnp.asarray(first_placement(), BF16)
    result = pl.pallas_call(
        functools.partial(body, depths, heights),
        out_shape=pltpu.VMEM((256, 128), BF16),
        in_specs=[pl.BlockSpec(memory_space=pltpu.HBM)] * 5,
        out_specs=pl.BlockSpec(memory_space=pltpu.VMEM),
        scratch_shapes=[
            pltpu.VMEM((4, 4, 8, 512), BF16),
            pltpu.VMEM((3, 3, 3, 4, 32), BF16),
            pltpu.VMEM((3, 3, 96, 64), BF16),
            pltpu.VMEM((3, 3, 192, 128), BF16),
            pltpu.VMEM((128, 4096), BF16),
            pltpu.VMEM((512, 128), F32),
            pltpu.VMEM((10, 14, 16, 128), BF16),
            pltpu.VMEM((10, 14, 16, 128), BF16),
            pltpu.VMEM((10, 14, 16, 128), BF16),
            pltpu.VMEM((128, 32), F32),
            pltpu.VMEM((2, 256, 256), BF16),
            pltpu.VMEM((4, 6, 128, 128), BF16),
            pltpu.VMEM((6, 256, 256), BF16),
            pltpu.VMEM((3, 4, 64, 128), BF16),
            pltpu.VMEM((3, 4, 192, 128), BF16),
            pltpu.VMEM((9, 128, 192), BF16),
            pltpu.VMEM((256, 128), F32),
            pltpu.VMEM((10, 3, 16, 128), BF16),
            pltpu.SemaphoreType.DMA((5,)),
            pltpu.SemaphoreType.DMA((26,)),
            pltpu.SemaphoreType.DMA((21,)),
            pltpu.SemaphoreType.REGULAR,
            pltpu.SemaphoreType.REGULAR,
            pltpu.SemaphoreType.REGULAR((2,)),
        ],
        compiler_params=pltpu.CompilerParams(
            collective_id=0, has_side_effects=True
        ),
        cost_estimate=pl.CostEstimate(flops=2 * 10**9, bytes_accessed=3 * 10**6, transcendentals=0),
        name="layers",
    )(volume, first, second.reshape(3, 3, 96, 64), third.reshape(3, 3, 192, 128), placement)
    return result.reshape(128, 1, 2, 128)


def solution(mesh):
    in_specs = (P(None, "depth", "height", None), P(), P(), P())
    out_specs = P(None, "depth", "height", None)
    local = functools.partial(shards, mesh.shape["depth"], mesh.shape["height"])
    return jax.shard_map(local, mesh=mesh, in_specs=in_specs, out_specs=out_specs, check_vma=False)
```

```python
import functools

import jax
import jax.numpy as jnp
import numpy as np
from jax import lax
from jax.experimental import pallas as pl
from jax.experimental.pallas import tpu as pltpu
from jax.sharding import PartitionSpec as P

MESH = pl.DeviceIdType.MESH
BF16 = jnp.bfloat16
F32 = jnp.float32
SLOPE = 0.3
RING = 8
SIDES = [(a, b) for b in (0, 1, -1) for a in (0, -1, 1) if (a, b) != (0, 0)]


def phase_matrix():
    cell = lax.broadcasted_iota(jnp.int32, (512, 512), 0)
    column = lax.broadcasted_iota(jnp.int32, (512, 512), 1)
    return jnp.where(cell == 4 * (column & 127) + (column >> 7), 1.0, 0.0).astype(BF16)


def first_placement():
    place = np.zeros((3, 3, 3, 4, 2, 2, 2, 2, 4, 4, 4, 4), np.float32)
    order = ((1, 2, 3, 0), (3, 0, 1, 2))
    for a, b, e, c, s, pd, ph, pw in np.ndindex(3, 3, 3, 4, 2, 2, 2, 2):
        place[a, b, e, c, s, pd, ph, pw, pd + a, ph + b, order[s].index(pw + e), c] = 1
    return np.pad(place.reshape(108, 4096), ((0, 20), (0, 0)))


def nt_dot(left, right):
    return lax.dot_general(left, right, (((1,), (1,)), ((), ())), preferred_element_type=F32)


def dot(left, right):
    return jnp.dot(left, right, preferred_element_type=F32)


def eye(size):
    rows = lax.broadcasted_iota(jnp.int32, (size, size), 0)
    columns = lax.broadcasted_iota(jnp.int32, (size, size), 1)
    return jnp.where(rows == columns, 1.0, 0.0).astype(BF16)


def before(value):
    lane = lax.broadcasted_iota(jnp.int32, value.shape, 1)
    return jnp.where(lane == 0, jnp.zeros_like(value), pltpu.roll(value, 1, 1))


def after(value):
    lane = lax.broadcasted_iota(jnp.int32, value.shape, 1)
    return jnp.where(lane == 127, jnp.zeros_like(value), pltpu.roll(value, 127, 1))


def leaky(value):
    return jnp.where(value > 0, value, SLOPE * value)


def span(shift, size, halo, received):
    if shift == 0:
        return pl.ds(halo, size)
    if received:
        return pl.ds(0, halo) if shift == 1 else pl.ds(halo + size, halo)
    return pl.ds(size, halo) if shift == 1 else pl.ds(halo, halo)


def body(
    depths, heights,
    volume, first, second, third, placement, out,
    x, k1, k2, k3, place, y, g, e0, e1, k1f, w1, f, w2, t, w3, of,
    passed, load_sem, send_sem, recv_sem, door, go, ready,
):
    di, hi = lax.axis_index("depth"), lax.axis_index("height")

    def within(a, b):
        return (di + a >= 0) & (di + a < depths) & (hi + b >= 0) & (hi + b < heights)

    loads = [
        pltpu.make_async_copy(source, target, load_sem.at[i])
        for i, (source, target) in enumerate(
            ((volume, x), (first, k1), (placement, place), (second, k2), (third, k3))
        )
    ]
    loads[0].start()

    rings = heights == 2 * RING
    late, source = (hi == RING - 1) & rings, (hi == RING) & rings
    relay, herald = (hi == 0) & rings, (hi == 1) & rings

    barrier = pltpu.get_barrier_semaphore()

    def greet(semaphore, a, b, condition):
        @pl.when(condition & within(a, b))
        def _():
            pl.semaphore_signal(semaphore, inc=1, device_id=(di + a, hi + b), device_id_type=MESH)

    greet(barrier, 0, 1 - RING, late)
    for a, b in SIDES:
        greet(barrier, a, b, jnp.logical_not({1: late, 0: relay, -1: herald}[b]))
    greet(barrier, 0, RING, relay)
    phase = phase_matrix()
    loads[0].wait()
    for load in loads[1:]:
        load.start()
    spread = dot(x[...].reshape(128, 512), phase)
    for i in range(4):
        y[pl.ds(i * 128, 128), :] = spread[:, i * 128 : (i + 1) * 128]
    for d in range(4):
        for h in range(8):
            g[3 + d, 3 + h] = y[pl.ds(d * 8 + h, 16, stride=32), :].astype(BF16)

    count_d = 1 + (di > 0).astype(jnp.int32) + (di < depths - 1).astype(jnp.int32)
    count_h = 1 + (hi > 0).astype(jnp.int32) + (hi < heights - 1).astype(jnp.int32)
    around = count_d * count_h - 1 + jnp.where(source, 1 - count_d, 0)
    pl.when(jnp.logical_not(relay))(lambda: pl.semaphore_wait(barrier, around))
    greet(go, 0, -1, herald)
    for a in (-1, 1):
        greet(ready.at[(1 - a) // 2], a, 0, source)
    for a in (0, -1, 1):
        greet(door, a, 1, late)
    pl.when(relay)(lambda: pl.semaphore_wait(go, 1))

    passing, relayed = [], []
    for i, a in enumerate((0, -1, 1)):
        copy = pltpu.make_async_remote_copy(
            src_ref=g.at[span(a, 4, 3, False), pl.ds(3, 3)],
            dst_ref=passed.at[span(a, 4, 3, True)],
            send_sem=send_sem.at[18 + i],
            recv_sem=recv_sem.at[18 + i],
            device_id=(di + a, hi - RING),
            device_id_type=MESH,
        )
        passing.append((a, copy))
        copy = pltpu.make_async_remote_copy(
            src_ref=passed.at[span(a, 4, 3, True)],
            dst_ref=g.at[span(a, 4, 3, True), pl.ds(11, 3)],
            send_sem=send_sem.at[21 + i],
            recv_sem=recv_sem.at[SIDES.index((a, -1))],
            device_id=(di, hi + RING - 1),
            device_id_type=MESH,
        )
        relayed.append((a, copy))

    pl.when(source)(passing[0][1].start)

    mate = {1: lax.rem(di, 2) == 0, -1: lax.rem(di, 2) == 1}
    shared = []
    for i, a in enumerate((-1, 1)):
        copy = pltpu.make_async_remote_copy(
            src_ref=g.at[span(a, 4, 3, False), pl.ds(0, 3)],
            dst_ref=g.at[span(a, 4, 3, True), pl.ds(0, 3)],
            send_sem=send_sem.at[24 + i],
            recv_sem=recv_sem.at[SIDES.index((a, 1))],
            device_id=(di + a, hi),
            device_id_type=MESH,
        )
        shared.append((source & mate[a], copy))

    halo = []
    for i, (a, b) in enumerate(SIDES):
        copy = pltpu.make_async_remote_copy(
            src_ref=g.at[span(a, 4, 3, False), span(b, 8, 3, False)],
            dst_ref=g.at[span(a, 4, 3, True), span(b, 8, 3, True)],
            send_sem=send_sem.at[i],
            recv_sem=recv_sem.at[i],
            device_id=(di + a, hi + b),
            device_id_type=MESH,
        )
        direct = within(a, b)
        if b == -1:
            direct &= jnp.logical_not(source)
        if b == 1 and a != 0:
            direct &= jnp.logical_not(late & mate[a])
        pl.when(direct)(copy.start)
        halo.append(((a, b), copy, direct))

    for a, copy in passing[1:]:
        @pl.when(source & within(a, 0))
        def _():
            pl.semaphore_wait(ready.at[(1 + a) // 2], 1)
            copy.start()

    def arrive(shift):
        for (a, b), copy, direct in halo:
            if b == shift:
                pl.when(within(-a, -b))(copy.wait_recv)
                if (a, b) == (0, 1):
                    for condition, share in shared:
                        pl.when(condition)(share.start)

    def row_copy(r, a, b, index):
        return pltpu.make_async_remote_copy(
            src_ref=t.at[1, 1 + r],
            dst_ref=t.at[1 - a, 1 + r if b is None else 3 - 3 * r],
            send_sem=send_sem.at[8 + 5 * r + index],
            recv_sem=recv_sem.at[8 + 5 * r + index],
            device_id=(di + a, hi if b is None else hi + b),
            device_id_type=MESH,
        )

    row_copies = []
    for r in range(2):
        side = [(a, 2 * r - 1, row_copy(r, a, 2 * r - 1, 2 + i)) for i, a in enumerate((0, -1, 1))]
        row_copies.append(side + [(a, 0, row_copy(r, a, None, i)) for i, a in enumerate((-1, 1))])

    for a, b in SIDES:
        @pl.when(jnp.logical_not(within(-a, -b)))
        def _():
            d1, h1 = span(a, 4, 3, True), span(b, 8, 3, True)
            g[d1, h1] = jnp.zeros((d1.size, h1.size, 16, 128), BF16)
            d2, h2 = span(a, 1, 1, True), span(b, 2, 1, True)
            t[d2, h2] = jnp.zeros((d2.size, h2.size, 64, 128), BF16)

    for load in loads[1:]:
        load.wait()
    k1f[...] = jnp.zeros_like(k1f)
    for i, (a, b, e) in enumerate(np.ndindex(3, 3, 3)):
        k1f[pl.ds(4 * i, 4), :] = k1[a, b, e].astype(F32)
    flat = nt_dot(eye(32), k1f[...].astype(BF16)).astype(BF16)
    for s in range(2):
        for p in range(0, 8, 4):
            wide = dot(flat, place[:, pl.ds((s * 8 + p) * 256, 1024)]).astype(BF16)
            for q in range(4):
                w1[s, pl.ds((p + q) * 32, 32), :] = wide[:, q * 256 : (q + 1) * 256]

    unit = eye(64)
    blank = jnp.zeros((32, 64), BF16)
    for a in range(3):
        for b in range(3):
            taps = k2[a, b].reshape(96, 64)
            turned = nt_dot(unit, jnp.concatenate([taps, blank, blank, taps], 0)).astype(BF16)
            for ph in range(2):
                for pw in range(2):
                    h = b + ph
                    w2[2 * a + h // 2, pl.ds(ph * 128 + pw * 64, 64), pl.ds(h % 2 * 128, 128)] = turned[
                        :, pw * 128 : (pw + 1) * 128
                    ]
        for ph, h in ((0, 3), (1, 0)):
            w2[2 * a + h // 2, pl.ds(ph * 128, 128), pl.ds(h % 2 * 128, 128)] = jnp.zeros((128, 128), BF16)

    unit = eye(128)
    for i in range(9):
        rows = k3[i // 3, i % 3].reshape(192, 128)
        w3[i] = nt_dot(unit, rows).astype(BF16)

    def widen(d0, depth, h0, height):
        here = pl.ds(d0, depth), pl.ds(h0, height)
        value = g[here].reshape(depth * height * 16, 128)
        row = lax.broadcasted_iota(jnp.int32, value.shape, 0) & 15
        shape = (depth, height, 16, 128)
        e0[here] = jnp.where(row >= 12, before(value), value).reshape(shape)
        e1[here] = jnp.where(row < 4, after(value), value).reshape(shape)

    def first_layer(hp):
        for dp in range(4):
            deep = 2 * di + dp - 1
            deep_in = (deep >= 0) & (deep < 2 * depths)
            halves = []
            for s, e in enumerate((e0, e1)):
                parts = [
                    e[pl.ds(2 * dp, 4), pl.ds(2 * (hp + j), 4)].reshape(256, 128) for j in range(2)
                ]
                sums = dot(w1[s], jnp.concatenate(parts, 1))
                halves.append(leaky(jnp.max(sums.reshape(8, 32, 256), axis=0)))
            for j in range(2):
                tall = 4 * hi + hp + j - 1
                keep = jnp.where(deep_in & (tall >= 0) & (tall < 4 * heights), 1.0, 0.0)
                p0, p1 = ((half[:, j * 128 : (j + 1) * 128] * keep).astype(BF16) for half in halves)
                for i, part in enumerate((before(p1), p0, p1, after(p0))):
                    f[dp, hp + j, pl.ds(32 * i, 32), :] = part

    def second_layer(hp, later):
        total = None
        for a in range(3):
            parts = [f[pd + a, pl.ds(hp, 2)].reshape(256, 128) for pd in range(2)]
            term = dot(w2[2 * a + later], jnp.concatenate(parts, 1))
            total = term if total is None else total + term
        return total

    @pl.when(relay)
    def _():
        pl.semaphore_wait(barrier, 1)
        for (a, arriving), (_, leaving) in zip(passing, relayed):
            @pl.when(within(-a, 0))
            def _():
                arriving.wait_recv()
                leaving.start()

    widen(3, 4, 3, 8)
    arrive(0)
    widen(0, 3, 3, 8)
    widen(7, 3, 3, 8)
    first_layer(2)

    def finish_row(r):
        half = second_layer(2, 1 - r)
        arrive(1 - 2 * r)
        widen(0, 10, 11 * r, 3)
        first_layer(4 * r)
        sums = second_layer(4 * r, r) + half
        sums = jnp.max(sums.reshape(4, 64, 256), axis=0)
        t[1, 1 + r] = leaky(jnp.maximum(sums[:, 0:128], sums[:, 128:256])).astype(BF16)
        if r == 0:
            pl.when(source)(lambda: pl.semaphore_wait(door, count_d))
        for a, b, copy in row_copies[r]:
            pl.when(within(a, b))(copy.start)

    @pl.when(source | late)
    def _():
        finish_row(1)
        finish_row(0)

    @pl.when(jnp.logical_not(source | late))
    def _():
        finish_row(0)
        finish_row(1)

    def spread_taps(d, h):
        value = t[d, h]
        return jnp.concatenate([before(value), value, after(value)], 0)

    def add_row(h, depths_here):
        for d in depths_here:
            places = [j for j in range(2) if 0 <= h - j <= 2]
            terms = dot(jnp.concatenate([w3[3 * d + h - j] for j in places], 0), spread_taps(d, h))
            for i, j in enumerate(places):
                term = terms[i * 128 : (i + 1) * 128]
                totals[j] = term if totals[j] is None else totals[j] + term

    def rows_arrive(r, side):
        for a, b, copy in row_copies[r]:
            if (b != 0) == side:
                pl.when(within(-a, -b))(copy.wait_recv)

    totals = [None, None]
    add_row(1, (1,))
    add_row(2, (1,))
    for condition, copy in shared:
        pl.when(condition)(copy.wait_send)
    for a, copy in passing:
        pl.when(source & within(a, 0))(copy.wait_send)
    for a, copy in relayed:
        pl.when(relay & within(-a, 0))(copy.wait_send)
    for _, copy, direct in halo:
        pl.when(direct)(copy.wait_send)
    rows_arrive(1, False)
    add_row(2, (0, 2))
    rows_arrive(0, True)
    add_row(3, (0, 1, 2))
    rows_arrive(0, False)
    add_row(1, (0, 2))
    of[pl.ds(1, 128, stride=2), :] = leaky(totals[1])
    for a, b, copy in row_copies[1]:
        pl.when(within(a, b))(copy.wait_send)
    rows_arrive(1, True)
    add_row(0, (0, 1, 2))
    of[pl.ds(0, 128, stride=2), :] = leaky(totals[0])

    out[...] = of[...].astype(BF16)
    for a, b, copy in row_copies[0]:
        pl.when(within(a, b))(copy.wait_send)


def shards(depths, heights, volume, first, second, third):
    placement = jnp.asarray(first_placement(), BF16)
    result = pl.pallas_call(
        functools.partial(body, depths, heights),
        out_shape=pltpu.VMEM((256, 128), BF16),
        in_specs=[pl.BlockSpec(memory_space=pltpu.HBM)] * 5,
        out_specs=pl.BlockSpec(memory_space=pltpu.VMEM),
        scratch_shapes=[
            pltpu.VMEM((4, 4, 8, 512), BF16),
            pltpu.VMEM((3, 3, 3, 4, 32), BF16),
            pltpu.VMEM((3, 3, 96, 64), BF16),
            pltpu.VMEM((3, 3, 192, 128), BF16),
            pltpu.VMEM((128, 4096), BF16),
            pltpu.VMEM((512, 128), F32),
            pltpu.VMEM((10, 14, 16, 128), BF16),
            pltpu.VMEM((10, 14, 16, 128), BF16),
            pltpu.VMEM((10, 14, 16, 128), BF16),
            pltpu.VMEM((128, 32), F32),
            pltpu.VMEM((2, 256, 256), BF16),
            pltpu.VMEM((4, 6, 128, 128), BF16),
            pltpu.VMEM((6, 256, 256), BF16),
            pltpu.VMEM((3, 4, 64, 128), BF16),
            pltpu.VMEM((9, 128, 192), BF16),
            pltpu.VMEM((256, 128), F32),
            pltpu.VMEM((10, 3, 16, 128), BF16),
            pltpu.SemaphoreType.DMA((5,)),
            pltpu.SemaphoreType.DMA((26,)),
            pltpu.SemaphoreType.DMA((21,)),
            pltpu.SemaphoreType.REGULAR,
            pltpu.SemaphoreType.REGULAR,
            pltpu.SemaphoreType.REGULAR((2,)),
        ],
        compiler_params=pltpu.CompilerParams(
            collective_id=0, has_side_effects=True
        ),
        cost_estimate=pl.CostEstimate(flops=2 * 10**9, bytes_accessed=3 * 10**6, transcendentals=0),
        name="layers",
    )(volume, first, second.reshape(3, 3, 96, 64), third.reshape(3, 3, 192, 128), placement)
    return result.reshape(128, 1, 2, 128)


def solution(mesh):
    in_specs = (P(None, "depth", "height", None), P(), P(), P())
    out_specs = P(None, "depth", "height", None)
    local = functools.partial(shards, mesh.shape["depth"], mesh.shape["height"])
    return jax.shard_map(local, mesh=mesh, in_specs=in_specs, out_specs=out_specs, check_vma=False)
```

```python
import functools

import jax
import jax.numpy as jnp
import numpy as np
from jax import lax
from jax.experimental import pallas as pl
from jax.experimental.pallas import tpu as pltpu
from jax.sharding import PartitionSpec as P

MESH = pl.DeviceIdType.MESH
BF16 = jnp.bfloat16
F32 = jnp.float32
SLOPE = 0.3
RING = 8
SIDES = [(a, b) for b in (0, 1, -1) for a in (0, -1, 1) if (a, b) != (0, 0)]


def phase_matrix():
    cell = lax.broadcasted_iota(jnp.int32, (512, 512), 0)
    column = lax.broadcasted_iota(jnp.int32, (512, 512), 1)
    return jnp.where(cell == 4 * (column & 127) + (column >> 7), 1.0, 0.0).astype(BF16)


def first_placement():
    place = np.zeros((3, 3, 3, 4, 2, 2, 2, 2, 4, 4, 4, 4), np.float32)
    order = ((1, 2, 3, 0), (3, 0, 1, 2))
    for a, b, e, c, s, pd, ph, pw in np.ndindex(3, 3, 3, 4, 2, 2, 2, 2):
        place[a, b, e, c, s, pd, ph, pw, pd + a, ph + b, order[s].index(pw + e), c] = 1
    return np.pad(place.reshape(108, 4096), ((0, 20), (0, 0)))


def nt_dot(left, right):
    return lax.dot_general(left, right, (((1,), (1,)), ((), ())), preferred_element_type=F32)


def dot(left, right):
    return jnp.dot(left, right, preferred_element_type=F32)


def eye(size):
    rows = lax.broadcasted_iota(jnp.int32, (size, size), 0)
    columns = lax.broadcasted_iota(jnp.int32, (size, size), 1)
    return jnp.where(rows == columns, 1.0, 0.0).astype(BF16)


def before(value):
    lane = lax.broadcasted_iota(jnp.int32, value.shape, 1)
    return jnp.where(lane == 0, jnp.zeros_like(value), pltpu.roll(value, 1, 1))


def after(value):
    lane = lax.broadcasted_iota(jnp.int32, value.shape, 1)
    return jnp.where(lane == 127, jnp.zeros_like(value), pltpu.roll(value, 127, 1))


def leaky(value):
    return jnp.where(value > 0, value, SLOPE * value)


def span(shift, size, halo, received):
    if shift == 0:
        return pl.ds(halo, size)
    if received:
        return pl.ds(0, halo) if shift == 1 else pl.ds(halo + size, halo)
    return pl.ds(size, halo) if shift == 1 else pl.ds(halo, halo)


def body(
    depths, heights,
    volume, first, second, third, placement, out,
    x, k1, k2, k3, place, y, g, e0, e1, k1f, w1, f, w2, t, w3, of,
    passed, load_sem, send_sem, recv_sem, door, go, ready,
):
    di, hi = lax.axis_index("depth"), lax.axis_index("height")

    def within(a, b):
        return (di + a >= 0) & (di + a < depths) & (hi + b >= 0) & (hi + b < heights)

    loads = [
        pltpu.make_async_copy(source, target, load_sem.at[i])
        for i, (source, target) in enumerate(
            ((volume, x), (first, k1), (placement, place), (second, k2), (third, k3))
        )
    ]

    rings = heights == 2 * RING
    late, source = (hi == RING - 1) & rings, (hi == RING) & rings
    relay, herald = (hi == 0) & rings, (hi == 1) & rings

    barrier = pltpu.get_barrier_semaphore()

    def greet(semaphore, a, b, condition):
        @pl.when(condition & within(a, b))
        def _():
            pl.semaphore_signal(semaphore, inc=1, device_id=(di + a, hi + b), device_id_type=MESH)

    greet(barrier, 0, 1 - RING, late)
    for a, b in SIDES:
        greet(barrier, a, b, jnp.logical_not({1: late, 0: relay, -1: herald}[b]))
    greet(barrier, 0, RING, relay)
    loads[0].start()

    phase = phase_matrix()
    loads[0].wait()
    for load in loads[1:]:
        load.start()
    spread = dot(x[...].reshape(128, 512), phase)
    for i in range(4):
        y[pl.ds(i * 128, 128), :] = spread[:, i * 128 : (i + 1) * 128]
    for d in range(4):
        for h in range(8):
            g[3 + d, 3 + h] = y[pl.ds(d * 8 + h, 16, stride=32), :].astype(BF16)

    count_d = 1 + (di > 0).astype(jnp.int32) + (di < depths - 1).astype(jnp.int32)
    count_h = 1 + (hi > 0).astype(jnp.int32) + (hi < heights - 1).astype(jnp.int32)
    around = count_d * count_h - 1 + jnp.where(source, 1 - count_d, 0)
    pl.when(jnp.logical_not(relay))(lambda: pl.semaphore_wait(barrier, around))
    greet(go, 0, -1, herald)
    for a in (-1, 1):
        greet(ready.at[(1 - a) // 2], a, 0, source)
    for a in (0, -1, 1):
        greet(door, a, 1, late)
    pl.when(relay)(lambda: pl.semaphore_wait(go, 1))

    passing, relayed = [], []
    for i, a in enumerate((0, -1, 1)):
        copy = pltpu.make_async_remote_copy(
            src_ref=g.at[span(a, 4, 3, False), pl.ds(3, 3)],
            dst_ref=passed.at[span(a, 4, 3, True)],
            send_sem=send_sem.at[18 + i],
            recv_sem=recv_sem.at[18 + i],
            device_id=(di + a, hi - RING),
            device_id_type=MESH,
        )
        passing.append((a, copy))
        copy = pltpu.make_async_remote_copy(
            src_ref=passed.at[span(a, 4, 3, True)],
            dst_ref=g.at[span(a, 4, 3, True), pl.ds(11, 3)],
            send_sem=send_sem.at[21 + i],
            recv_sem=recv_sem.at[SIDES.index((a, -1))],
            device_id=(di, hi + RING - 1),
            device_id_type=MESH,
        )
        relayed.append((a, copy))

    pl.when(source)(passing[0][1].start)

    mate = {1: lax.rem(di, 2) == 0, -1: lax.rem(di, 2) == 1}
    shared = []
    for i, a in enumerate((-1, 1)):
        copy = pltpu.make_async_remote_copy(
            src_ref=g.at[span(a, 4, 3, False), pl.ds(0, 3)],
            dst_ref=g.at[span(a, 4, 3, True), pl.ds(0, 3)],
            send_sem=send_sem.at[24 + i],
            recv_sem=recv_sem.at[SIDES.index((a, 1))],
            device_id=(di + a, hi),
            device_id_type=MESH,
        )
        shared.append((source & mate[a], copy))

    halo = []
    for i, (a, b) in enumerate(SIDES):
        copy = pltpu.make_async_remote_copy(
            src_ref=g.at[span(a, 4, 3, False), span(b, 8, 3, False)],
            dst_ref=g.at[span(a, 4, 3, True), span(b, 8, 3, True)],
            send_sem=send_sem.at[i],
            recv_sem=recv_sem.at[i],
            device_id=(di + a, hi + b),
            device_id_type=MESH,
        )
        direct = within(a, b)
        if b == -1:
            direct &= jnp.logical_not(source)
        if b == 1 and a != 0:
            direct &= jnp.logical_not(late & mate[a])
        pl.when(direct)(copy.start)
        halo.append(((a, b), copy, direct))

    for a, copy in passing[1:]:
        @pl.when(source & within(a, 0))
        def _():
            pl.semaphore_wait(ready.at[(1 + a) // 2], 1)
            copy.start()

    def arrive(shift):
        for (a, b), copy, direct in halo:
            if b == shift:
                pl.when(within(-a, -b))(copy.wait_recv)
                if (a, b) == (0, 1):
                    for condition, share in shared:
                        pl.when(condition)(share.start)

    def row_copy(r, a, b, index):
        return pltpu.make_async_remote_copy(
            src_ref=t.at[1, 1 + r],
            dst_ref=t.at[1 - a, 1 + r if b is None else 3 - 3 * r],
            send_sem=send_sem.at[8 + 5 * r + index],
            recv_sem=recv_sem.at[8 + 5 * r + index],
            device_id=(di + a, hi if b is None else hi + b),
            device_id_type=MESH,
        )

    row_copies = []
    for r in range(2):
        side = [(a, 2 * r - 1, row_copy(r, a, 2 * r - 1, 2 + i)) for i, a in enumerate((0, -1, 1))]
        row_copies.append(side + [(a, 0, row_copy(r, a, None, i)) for i, a in enumerate((-1, 1))])

    for a, b in SIDES:
        @pl.when(jnp.logical_not(within(-a, -b)))
        def _():
            d1, h1 = span(a, 4, 3, True), span(b, 8, 3, True)
            g[d1, h1] = jnp.zeros((d1.size, h1.size, 16, 128), BF16)
            d2, h2 = span(a, 1, 1, True), span(b, 2, 1, True)
            t[d2, h2] = jnp.zeros((d2.size, h2.size, 64, 128), BF16)

    for load in loads[1:]:
        load.wait()
    k1f[...] = jnp.zeros_like(k1f)
    for i, (a, b, e) in enumerate(np.ndindex(3, 3, 3)):
        k1f[pl.ds(4 * i, 4), :] = k1[a, b, e].astype(F32)
    flat = nt_dot(eye(32), k1f[...].astype(BF16)).astype(BF16)
    for s in range(2):
        for p in range(0, 8, 4):
            wide = dot(flat, place[:, pl.ds((s * 8 + p) * 256, 1024)]).astype(BF16)
            for q in range(4):
                w1[s, pl.ds((p + q) * 32, 32), :] = wide[:, q * 256 : (q + 1) * 256]

    unit = eye(64)
    blank = jnp.zeros((32, 64), BF16)
    for a in range(3):
        for b in range(3):
            taps = k2[a, b].reshape(96, 64)
            turned = nt_dot(unit, jnp.concatenate([taps, blank, blank, taps], 0)).astype(BF16)
            for ph in range(2):
                for pw in range(2):
                    h = b + ph
                    w2[2 * a + h // 2, pl.ds(ph * 128 + pw * 64, 64), pl.ds(h % 2 * 128, 128)] = turned[
                        :, pw * 128 : (pw + 1) * 128
                    ]
        for ph, h in ((0, 3), (1, 0)):
            w2[2 * a + h // 2, pl.ds(ph * 128, 128), pl.ds(h % 2 * 128, 128)] = jnp.zeros((128, 128), BF16)

    unit = eye(128)
    for i in range(9):
        rows = k3[i // 3, i % 3].reshape(192, 128)
        w3[i] = nt_dot(unit, rows).astype(BF16)

    def widen(d0, depth, h0, height):
        here = pl.ds(d0, depth), pl.ds(h0, height)
        value = g[here].reshape(depth * height * 16, 128)
        row = lax.broadcasted_iota(jnp.int32, value.shape, 0) & 15
        shape = (depth, height, 16, 128)
        e0[here] = jnp.where(row >= 12, before(value), value).reshape(shape)
        e1[here] = jnp.where(row < 4, after(value), value).reshape(shape)

    def first_layer(hp):
        for dp in range(4):
            deep = 2 * di + dp - 1
            deep_in = (deep >= 0) & (deep < 2 * depths)
            halves = []
            for s, e in enumerate((e0, e1)):
                parts = [
                    e[pl.ds(2 * dp, 4), pl.ds(2 * (hp + j), 4)].reshape(256, 128) for j in range(2)
                ]
                sums = dot(w1[s], jnp.concatenate(parts, 1))
                halves.append(leaky(jnp.max(sums.reshape(8, 32, 256), axis=0)))
            for j in range(2):
                tall = 4 * hi + hp + j - 1
                keep = jnp.where(deep_in & (tall >= 0) & (tall < 4 * heights), 1.0, 0.0)
                p0, p1 = ((half[:, j * 128 : (j + 1) * 128] * keep).astype(BF16) for half in halves)
                for i, part in enumerate((before(p1), p0, p1, after(p0))):
                    f[dp, hp + j, pl.ds(32 * i, 32), :] = part

    def second_layer(hp, later):
        total = None
        for a in range(3):
            parts = [f[pd + a, pl.ds(hp, 2)].reshape(256, 128) for pd in range(2)]
            term = dot(w2[2 * a + later], jnp.concatenate(parts, 1))
            total = term if total is None else total + term
        return total

    @pl.when(relay)
    def _():
        pl.semaphore_wait(barrier, 1)
        for (a, arriving), (_, leaving) in zip(passing, relayed):
            @pl.when(within(-a, 0))
            def _():
                arriving.wait_recv()
                leaving.start()

    widen(3, 4, 3, 8)
    arrive(0)
    widen(0, 3, 3, 8)
    widen(7, 3, 3, 8)
    first_layer(2)

    def finish_row(r):
        half = second_layer(2, 1 - r)
        arrive(1 - 2 * r)
        widen(0, 10, 11 * r, 3)
        first_layer(4 * r)
        sums = second_layer(4 * r, r) + half
        sums = jnp.max(sums.reshape(4, 64, 256), axis=0)
        t[1, 1 + r] = leaky(jnp.maximum(sums[:, 0:128], sums[:, 128:256])).astype(BF16)
        if r == 0:
            pl.when(source)(lambda: pl.semaphore_wait(door, count_d))
        for a, b, copy in row_copies[r]:
            pl.when(within(a, b))(copy.start)

    @pl.when(source | late)
    def _():
        finish_row(1)
        finish_row(0)

    @pl.when(jnp.logical_not(source | late))
    def _():
        finish_row(0)
        finish_row(1)

    def spread_taps(d, h):
        value = t[d, h]
        return jnp.concatenate([before(value), value, after(value)], 0)

    def add_row(h, depths_here):
        for d in depths_here:
            places = [j for j in range(2) if 0 <= h - j <= 2]
            terms = dot(jnp.concatenate([w3[3 * d + h - j] for j in places], 0), spread_taps(d, h))
            for i, j in enumerate(places):
                term = terms[i * 128 : (i + 1) * 128]
                totals[j] = term if totals[j] is None else totals[j] + term

    def rows_arrive(r, side):
        for a, b, copy in row_copies[r]:
            if (b != 0) == side:
                pl.when(within(-a, -b))(copy.wait_recv)

    totals = [None, None]
    add_row(1, (1,))
    add_row(2, (1,))
    for condition, copy in shared:
        pl.when(condition)(copy.wait_send)
    for a, copy in passing:
        pl.when(source & within(a, 0))(copy.wait_send)
    for a, copy in relayed:
        pl.when(relay & within(-a, 0))(copy.wait_send)
    for _, copy, direct in halo:
        pl.when(direct)(copy.wait_send)
    rows_arrive(1, False)
    add_row(2, (0, 2))
    rows_arrive(0, True)
    add_row(3, (0, 1, 2))
    rows_arrive(0, False)
    add_row(1, (0, 2))
    of[pl.ds(1, 128, stride=2), :] = leaky(totals[1])
    for a, b, copy in row_copies[1]:
        pl.when(within(a, b))(copy.wait_send)
    rows_arrive(1, True)
    add_row(0, (0, 1, 2))
    of[pl.ds(0, 128, stride=2), :] = leaky(totals[0])

    out[...] = of[...].astype(BF16)
    for a, b, copy in row_copies[0]:
        pl.when(within(a, b))(copy.wait_send)


def shards(depths, heights, volume, first, second, third):
    placement = jnp.asarray(first_placement(), BF16)
    result = pl.pallas_call(
        functools.partial(body, depths, heights),
        out_shape=pltpu.VMEM((256, 128), BF16),
        in_specs=[pl.BlockSpec(memory_space=pltpu.HBM)] * 5,
        out_specs=pl.BlockSpec(memory_space=pltpu.VMEM),
        scratch_shapes=[
            pltpu.VMEM((4, 4, 8, 512), BF16),
            pltpu.VMEM((3, 3, 3, 4, 32), BF16),
            pltpu.VMEM((3, 3, 96, 64), BF16),
            pltpu.VMEM((3, 3, 192, 128), BF16),
            pltpu.VMEM((128, 4096), BF16),
            pltpu.VMEM((512, 128), F32),
            pltpu.VMEM((10, 14, 16, 128), BF16),
            pltpu.VMEM((10, 14, 16, 128), BF16),
            pltpu.VMEM((10, 14, 16, 128), BF16),
            pltpu.VMEM((128, 32), F32),
            pltpu.VMEM((2, 256, 256), BF16),
            pltpu.VMEM((4, 6, 128, 128), BF16),
            pltpu.VMEM((6, 256, 256), BF16),
            pltpu.VMEM((3, 4, 64, 128), BF16),
            pltpu.VMEM((9, 128, 192), BF16),
            pltpu.VMEM((256, 128), F32),
            pltpu.VMEM((10, 3, 16, 128), BF16),
            pltpu.SemaphoreType.DMA((5,)),
            pltpu.SemaphoreType.DMA((26,)),
            pltpu.SemaphoreType.DMA((21,)),
            pltpu.SemaphoreType.REGULAR,
            pltpu.SemaphoreType.REGULAR,
            pltpu.SemaphoreType.REGULAR((2,)),
        ],
        compiler_params=pltpu.CompilerParams(
            collective_id=0, has_side_effects=True
        ),
        cost_estimate=pl.CostEstimate(flops=2 * 10**9, bytes_accessed=3 * 10**6, transcendentals=0),
        name="layers",
    )(volume, first, second.reshape(3, 3, 96, 64), third.reshape(3, 3, 192, 128), placement)
    return result.reshape(128, 1, 2, 128)


def solution(mesh):
    in_specs = (P(None, "depth", "height", None), P(), P(), P())
    out_specs = P(None, "depth", "height", None)
    local = functools.partial(shards, mesh.shape["depth"], mesh.shape["height"])
    return jax.shard_map(local, mesh=mesh, in_specs=in_specs, out_specs=out_specs, check_vma=False)
```
